128 devices in a mesh: src: 32 (over x, z, core), tgt: 4 (over y).
Axes of the slice: x: 4, y: 4, z: 4, core: 2. Of those that a mesh axis runs over, the one named last changes fastest.
Arguments:
- source_embed: bfloat16 [16384, 768], P('src'), may hold values from -16 to 16
- target_embed: bfloat16 [8192, 768], P(('tgt', 'src')), may hold values from -6 to 6
- source_mass: float32 [16384], P('src'), may hold values from 0.3 to 3
- target_mass: float32 [8192], P('tgt'), may hold values from 0.3 to 3
Outputs:
- readout: float32 [16384, 768], P('src')
- source_potential: float32 [16384], P('src')
- target_potential: float32 [8192], P('tgt')
The draws below stay inside these ranges and needn't reach their ends.
All inputs are finite; a program needn't handle non-finite values.
Results may differ from the reference program's by a relative error of at most 0.0028.
Values may be sent and summed in bfloat16 or wider, within the bound.
A program may use at most 64 MiB of HBM per device.

```python
import math
import jax
import jax.numpy as jnp
from jax import lax

D = 768
ITERS = 3
SOURCES = 16384
TARGETS = 8192


def normal_targets(key):
    return jnp.clip(jax.random.normal(key, (TARGETS, D), jnp.float32), -6.0, 6.0)


def draw_target_embed(key, part):
    base = normal_targets(key)
    values = base
    return values.astype(jnp.bfloat16)


def draw_source_embed(key, part):
    key = jax.random.fold_in(key, 5)
    own = jnp.clip(jax.random.normal(key, (SOURCES, D), jnp.float32), -6.0, 6.0)
    return own.astype(jnp.bfloat16)


def block_levels(key, shape, pieces, low, largest):
    loudness, own = 1.0, jax.random.fold_in(key, 6)
    for axis_at, blocks in pieces:
        draws = jnp.exp(jax.random.uniform(jax.random.fold_in(own, axis_at), (blocks,), jnp.float32, low / len(pieces), largest / len(pieces)))
        loudness = loudness * jnp.repeat(draws, shape[axis_at] // blocks).reshape([-1 if axis == axis_at else 1 for axis in range(len(shape))])
    return loudness


def setup_inputs(seed: int = 0) -> dict:
    splits = jax.random.split(jax.random.key(seed), 5)
    source_embed = draw_source_embed(jax.random.fold_in(splits[4], 71), 0)
    target_embed = draw_target_embed(jax.random.fold_in(splits[4], 71), 0)
    source_mass = jnp.clip(jnp.exp(math.log(3.0) - 2.3025851 * jax.random.uniform(splits[2], (SOURCES,), jnp.float32) ** block_levels(splits[2], (SOURCES,), ((0, 32),), -0.2, 0.2)), 0.3, 3.0)
    target_mass = jnp.clip(jnp.exp(math.log(3.0) - 2.3025851 * jax.random.uniform(splits[3], (TARGETS,), jnp.float32) ** block_levels(splits[3], (TARGETS,), ((0, 4),), -0.2, 0.2)), 0.3, 3.0)
    return {"source_embed": source_embed, "target_embed": target_embed, "source_mass": source_mass, "target_mass": target_mass}


def block_scores(sources, block, scale):
    return jnp.dot(sources, block.T, preferred_element_type=jnp.float32) * scale

def row_pass(sources, tgt_blocks, potential_g, scale):
    rows = sources.shape[0]

    def advance(carry, items):
        block, shift = items
        scores = block_scores(sources, block, scale) + shift[None, :]
        peak = jnp.maximum(carry[0], lax.optimization_barrier(jnp.max(scores, axis=1)))
        total = carry[1] * jnp.exp(carry[0] - peak) + lax.optimization_barrier(jnp.sum(jnp.exp(scores - peak[:, None]), axis=1))
        return ((peak, total), None)
    start = (jnp.full((rows,), -1e+30, jnp.float32), jnp.zeros((rows,), jnp.float32))
    return lax.scan(advance, start, (tgt_blocks, potential_g))[0]

def column_pass(sources, tgt_blocks, potential_f, scale):

    def single(block):
        scores = block_scores(sources, block, scale) + potential_f[:, None]
        peak = lax.optimization_barrier(jnp.max(scores, axis=0))
        return peak + jnp.log(lax.optimization_barrier(jnp.sum(jnp.exp(scores - peak[None, :]), axis=0)))
    return lax.map(single, tgt_blocks)

def reference(source_embed, target_embed, source_mass, target_mass):
    scale = 2.0 / math.sqrt(D)
    width = 512 if TARGETS % 512 == 0 else TARGETS
    count = TARGETS // width
    tgt_blocks = target_embed.reshape(count, width, D)
    log_a = jnp.log(source_mass)
    log_b = jnp.log(target_mass).reshape(count, width)
    potential_g = jnp.zeros((count, width), jnp.float32)
    potential_f = jnp.zeros((SOURCES,), jnp.float32)
    for step in range(ITERS):
        peak, total = row_pass(source_embed, tgt_blocks, potential_g, scale)
        potential_f = log_a - (peak + jnp.log(total))
        potential_g = log_b - column_pass(source_embed, tgt_blocks, potential_f, scale)
    offset = potential_f - log_a

    def gather_step(carry, items):
        block, shift = items
        weights = jnp.exp(block_scores(source_embed, block, scale) + shift[None, :] + offset[:, None])
        numer = carry[0] + jnp.dot(weights.astype(jnp.bfloat16), block, preferred_element_type=jnp.float32)
        return ((numer, carry[1] + lax.optimization_barrier(jnp.sum(weights, axis=1))), None)
    start = (jnp.zeros((SOURCES, D), jnp.float32), jnp.zeros((SOURCES,), jnp.float32))
    numerator, mass = lax.scan(gather_step, start, (tgt_blocks, potential_g))[0]
    readout = numerator / mass[:, None]
    return (readout, potential_f, potential_g.reshape(TARGETS))
```

```python
import functools
import math

import jax
import jax.numpy as jnp
from jax import lax
from jax.experimental import pallas as pl
from jax.experimental.pallas import tpu as pltpu
from jax.sharding import PartitionSpec as P

D = 768
HALF = D // 2
ITERS = 3
MESH = pl.DeviceIdType.MESH
SCALE = 2.0 / math.sqrt(D) * math.log2(math.e)
LN2 = math.log(2.0)
NT = (((1,), (1,)), ((), ()))
F32 = jnp.float32


def place():
    s = lax.axis_index("src")
    return s // 8, lax.axis_index("tgt"), (s // 2) % 4, s % 2


def device(x, y, z, c):
    return ((x * 4 + z) * 2 + c, y)


def row_peers(at):
    x, y, z, c = at
    peers = [
        (x, (y + step) % 4, z, (c + other) % 2) for step in (2, 1, 3) for other in (1, 0)
    ]
    return peers + [(x, y, z, 1 - c)]


def column_peers(at):
    x, y, z, c = at
    steps = [(a, b) for a in range(4) for b in range(4) if a or b]
    steps.sort(key=lambda t: -(min(t[0], 4 - t[0]) + min(t[1], 4 - t[1])))
    return [((x + a) % 4, y, (z + b) % 4, c) for a, b in steps]


def remote(src, dst, send, recv, to):
    return pltpu.make_async_remote_copy(
        src_ref=src,
        dst_ref=dst,
        send_sem=send,
        recv_sem=recv,
        device_id=device(*to),
        device_id_type=MESH,
    )


def gather_steps(targets, at, planes, send, recv, started):
    x, y, z, c = at
    copies = {}

    def go(h, k, first, second, low, rows, axis, step):
        a, b = (first, second) if h == 0 else (second, first)
        row = pl.multiple_of(((x + a) % 4 * 4 + (z + b) % 4) * 64 + low, 32)
        block = targets.at[c, planes, pl.ds(row, rows), pl.ds(h * HALF, HALF)]
        along_x = (axis == 1) == (h == 0)
        to = ((x + step) % 4, y, z, c) if along_x else (x, y, (z + step) % 4, c)
        copy = remote(block, block, send.at[h, k], recv.at[h, k], to)
        copy.start()
        copies[h, k] = copy
        started.append(copy)

    def second_axis(h, b, first):
        go(h, 4 + 4 * b, first, 0, 0, 64, 2, 1)
        go(h, 5 + 4 * b, first, 0, 0, 64, 2, -1)

    def forward(h, b, first):
        copies[h, 4 + 4 * b].wait_recv()
        go(h, 6 + 4 * b, first, -1, 0, 32, 2, 1)
        copies[h, 5 + 4 * b].wait_recv()
        go(h, 7 + 4 * b, first, 1, 32, 32, 2, -1)

    both = (0, 1)
    for h in both:
        go(h, 0, 0, 0, 0, 64, 1, 1)
        go(h, 1, 0, 0, 0, 64, 1, -1)
    for h in both:
        second_axis(h, 0, 0)
    yield
    for h in both:
        copies[h, 0].wait_recv()
        go(h, 2, -1, 0, 0, 32, 1, 1)
        second_axis(h, 1, -1)
        copies[h, 1].wait_recv()
        go(h, 3, 1, 0, 32, 32, 1, -1)
        second_axis(h, 2, 1)
    yield
    for h in both:
        forward(h, 0, 0)
    for h in both:
        copies[h, 2].wait_recv()
        copies[h, 3].wait_recv()
        second_axis(h, 3, 2)
    yield
    for b, first in ((1, -1), (2, 1)):
        for h in both:
            forward(h, b, first)
    yield
    for h in both:
        forward(h, 3, 2)
    yield
    for b in range(4):
        for h in both:
            copies[h, 6 + 4 * b].wait_recv()
            copies[h, 7 + 4 * b].wait_recv()


def combine(parts):
    peak = functools.reduce(jnp.maximum, parts)
    return peak + jnp.log2(functools.reduce(jnp.add, [jnp.exp2(p - peak) for p in parts]))


def row_pass(scores, g, out):
    lane = lax.broadcasted_iota(jnp.int32, (8, 128), 1)
    sub = lax.broadcasted_iota(jnp.int32, (8, 128), 0)
    shifts = [jnp.broadcast_to(g[k : k + 1, :], (8, 128)) for k in range(8)]

    def block(q, _):
        def group(i, acc):
            r = pl.multiple_of(q * 128 + i * 8, 8)
            xs = [scores[pl.ds(r, 8), pl.ds(128 * k, 128)] + shifts[k] for k in range(8)]
            peak = jnp.max(functools.reduce(jnp.maximum, xs), axis=1, keepdims=True)
            total = functools.reduce(jnp.add, [jnp.exp2(x - peak) for x in xs])
            value = peak + jnp.log2(jnp.sum(total, axis=1, keepdims=True))
            return jnp.where(lane - i * 8 == sub, value, acc)

        acc = lax.fori_loop(0, 16, group, jnp.zeros((8, 128), F32), unroll=16)
        out[pl.ds(q, 1), :] = jnp.sum(acc, axis=0, keepdims=True)
        return 0

    lax.fori_loop(0, 8, block, 0, unroll=2)


def spread(values, out):
    for q in range(values.shape[0]):
        out[pl.ds(q * 128, 128), :] = jnp.broadcast_to(values[q : q + 1, :], (128, 128)).T


def column_pass(scores, f_rows, out):
    def peaks(i, carry):
        r = pl.multiple_of(i * 8, 8)
        f = f_rows[pl.ds(r, 8), :]
        return tuple(
            jnp.maximum(carry[k], scores[pl.ds(r, 8), pl.ds(128 * k, 128)] + f)
            for k in range(8)
        )

    start = tuple(jnp.full((8, 128), -1e30, F32) for _ in range(8))
    top = lax.fori_loop(0, 128, peaks, start, unroll=16)
    top = [jnp.broadcast_to(jnp.max(t, axis=0, keepdims=True), (8, 128)) for t in top]

    def sums(i, carry):
        r = pl.multiple_of(i * 8, 8)
        f = f_rows[pl.ds(r, 8), :]
        return tuple(
            carry[k] + jnp.exp2(scores[pl.ds(r, 8), pl.ds(128 * k, 128)] + f - top[k])
            for k in range(8)
        )

    start = tuple(jnp.zeros((8, 128), F32) for _ in range(8))
    total = lax.fori_loop(0, 128, sums, start, unroll=16)
    for k in range(8):
        out[k : k + 1, :] = top[k][0:1] + jnp.log2(jnp.sum(total[k], axis=0, keepdims=True))


def kernel(
    source_ref, target_ref, a_ref, b_ref, readout_ref, f_ref, g_ref,
    sources, targets, masses, scores, wide, f_rows, mass_rows, row_buf, column_buf, g_buf,
    own_send, own_recv, far_send, far_recv, y_send, y_recv, in_send, in_recv,
    row_send, row_recv, column_send, column_recv, g_send, g_recv, core_send, core_recv,
):
    at = place()
    x, y, z, c = at
    rows, columns = row_peers(at), column_peers(at)
    barrier = pltpu.get_barrier_semaphore()
    for peer in columns + rows:
        pl.semaphore_signal(barrier, inc=1, device_id=device(*peer), device_id_type=MESH)
    pl.semaphore_wait(barrier, len(columns) + len(rows))

    sibling = (x, y, z, 1 - c)
    started = []
    own_rows = pl.ds(pl.multiple_of((x * 4 + z) * 64, 64), 64)
    half_rows = pl.ds(pl.multiple_of(c * 512, 512), 512)
    targets[c, 0, own_rows, :] = target_ref[...]
    sources[half_rows, :] = source_ref[...]
    masses[c] = a_ref[...]

    own = gather_steps(targets, at, pl.ds(0, 1), own_send, own_recv, started)
    next(own)
    crossings = []
    for k, step in enumerate((1, 3, 2)):
        dst = targets.at[c, 4 - step, own_rows]
        copy = remote(target_ref, dst, y_send.at[k], y_recv.at[k], (x, (y + step) % 4, z, c))
        copy.start()
        crossings.append(copy)
    inner = [
        remote(source_ref, sources.at[half_rows], in_send.at[0], in_recv.at[0], sibling),
        remote(a_ref, masses.at[c], in_send.at[1], in_recv.at[1], sibling),
    ]
    for copy in inner:
        copy.start()
    started += crossings + inner
    for _ in own:
        pass
    for copy in crossings:
        copy.wait_recv()
    far = gather_steps(targets, at, pl.ds(1, 3), far_send, far_recv, started)
    for _ in far:
        pass

    for copy in inner:
        copy.wait_recv()
    passed = []
    for k in range(8):
        part = targets.at[c, k // 2, pl.ds(k % 2 * 512, 512)]
        copy = remote(part, part, core_send.at[k], core_recv.at[k], sibling)
        copy.start()
        passed.append(copy)
    started += passed

    log_a = jnp.log2(jnp.concatenate([masses[0], masses[1]], axis=0))
    left = lax.broadcasted_iota(jnp.int32, (8, 128), 1) < 64
    even, odd = b_ref[pl.ds(0, 8, stride=2), :], b_ref[pl.ds(1, 8, stride=2), :]
    log_b = jnp.log2(
        jnp.where(
            c == 0,
            jnp.where(left, even, pltpu.roll(odd, 64, 1)),
            jnp.where(left, pltpu.roll(even, 64, 1), odd),
        )
    )

    for k in range(4):
        scores[:, k * 256 : (k + 1) * 256] = (
            lax.dot_general(
                sources[...],
                targets[c, 0, k * 256 : (k + 1) * 256, :],
                NT,
                preferred_element_type=F32,
            )
            * SCALE
        )

    def exchange(buf, me, peers, send, recv):
        for peer in peers:
            remote(buf.at[me], buf.at[me], send, recv, peer).start()

    def drain(buf, peers, sem):
        every = buf.at[pl.ds(0, len(peers))]
        pltpu.make_async_copy(every, every, sem).wait()

    g = jnp.zeros((8, 128), F32)
    row_me, column_me = y * 2 + c, x * 4 + z
    for it in range(ITERS):
        row_pass(scores, g, row_buf.at[it, row_me])
        exchange(row_buf.at[it], row_me, rows, row_send.at[it], row_recv.at[it])
        drain(row_buf.at[it], rows, row_recv.at[it])
        lse = combine([row_buf[it, k] for k in range(8)])
        f = log_a - lse
        spread(f, f_rows)
        column_pass(scores, f_rows, column_buf.at[it, column_me])
        exchange(column_buf.at[it], column_me, columns, column_send.at[it], column_recv.at[it])
        drain(column_buf.at[it], columns, column_recv.at[it])
        g = log_b - combine([column_buf[it, k] for k in range(16)])

    g_buf[c, 0] = g
    for other in (1, 0):
        for step in (2, 1, 3, 0):
            if step or other:
                to = (x, (y + step) % 4, z, (c + other) % 2)
                dst = g_buf.at[c, (4 - step) % 4]
                remote(g_buf.at[c, 0], dst, g_send, g_recv, to).start()
    every = row_buf.at[0, pl.ds(0, 7)]
    pltpu.make_async_copy(every, every, g_recv).wait()
    for copy in passed:
        copy.wait_recv()

    f_ref[...] = jnp.where(c == 0, f[0:4], f[4:8]) * LN2
    g0, g1 = g_buf[0, 0] * LN2, g_buf[1, 0] * LN2
    g_ref[pl.ds(0, 8, stride=2), :] = jnp.where(left, g0, pltpu.roll(g1, 64, 1))
    g_ref[pl.ds(1, 8, stride=2), :] = jnp.where(left, pltpu.roll(g0, 64, 1), g1)

    spread(jnp.where(c == 0, -lse[0:4], -lse[4:8]), f_rows)
    for k in range(8):
        wide[k] = (
            lax.dot_general(
                source_ref[...], targets[k // 4, k % 4], NT, preferred_element_type=F32
            )
            * SCALE
        )
    readout_ref[...] = jnp.zeros_like(readout_ref)
    mass_rows[...] = jnp.zeros_like(mass_rows)

    def part(k, _):
        base = f_rows[0:512, :]
        mass = mass_rows[...]
        weights = []
        for q in range(8):
            shift = g_buf[k // 4, k % 4, q : q + 1, :]
            w = jnp.exp2(wide[k, :, pl.ds(q * 128, 128)] + base + shift)
            mass = mass + w
            weights.append(w)
        mass_rows[...] = mass
        low = jnp.concatenate(weights, axis=1).astype(jnp.bfloat16)
        readout_ref[...] += jnp.dot(low, targets[k // 4, k % 4], preferred_element_type=F32)
        return 0

    lax.fori_loop(0, 8, part, 0)
    readout_ref[...] = readout_ref[...] / jnp.sum(mass_rows[...], axis=1, keepdims=True)

    for copy in started:
        copy.wait_send()
    for it in range(ITERS):
        drain(row_buf.at[it], rows, row_send.at[it])
        drain(column_buf.at[it], columns, column_send.at[it])
    pltpu.make_async_copy(every, every, g_send).wait()


def shards(source_embed, target_embed, source_mass, target_mass):
    vmem, dma = pltpu.VMEM, pltpu.SemaphoreType.DMA
    bf16 = jnp.bfloat16
    readout, f, g = pl.pallas_call(
        kernel,
        out_shape=(
            jax.ShapeDtypeStruct((512, D), F32),
            jax.ShapeDtypeStruct((4, 128), F32),
            jax.ShapeDtypeStruct((16, 128), F32),
        ),
        in_specs=[pl.BlockSpec(memory_space=vmem)] * 4,
        out_specs=(pl.BlockSpec(memory_space=vmem),) * 3,
        scratch_shapes=[
            vmem((1024, D), bf16),
            vmem((2, 4, 1024, D), bf16),
            vmem((2, 4, 128), F32),
            vmem((1024, 1024), F32),
            vmem((8, 512, 1024), F32),
            vmem((1024, 128), F32),
            vmem((512, 128), F32),
            vmem((ITERS, 8, 8, 128), F32),
            vmem((ITERS, 16, 8, 128), F32),
            vmem((2, 4, 8, 128), F32),
            dma((2, 20)),
            dma((2, 20)),
            dma((2, 20)),
            dma((2, 20)),
            dma((3,)),
            dma((3,)),
            dma((2,)),
            dma((2,)),
            dma((ITERS,)),
            dma((ITERS,)),
            dma((ITERS,)),
            dma((ITERS,)),
            dma(()),
            dma(()),
            dma((8,)),
            dma((8,)),
        ],
        name="sinkhorn",
        compiler_params=pltpu.CompilerParams(
            collective_id=0, has_side_effects=True, vmem_limit_bytes=56 << 20
        ),
    )(source_embed, target_embed, source_mass.reshape(4, 128), target_mass.reshape(16, 128))
    return readout, f.reshape(512), g.reshape(2048)


def solution(mesh):
    placed = (P("src", None), P(("tgt", "src"), None), P("src"), P("tgt"))
    return jax.shard_map(
        shards,
        mesh=mesh,
        in_specs=placed,
        out_specs=(P("src", None), P("src"), P("tgt")),
        check_vma=False,
    )
```

```python
import functools
import math

import jax
import jax.numpy as jnp
from jax import lax
from jax.experimental import pallas as pl
from jax.experimental.pallas import tpu as pltpu
from jax.sharding import PartitionSpec as P

D = 768
ITERS = 3
MESH = pl.DeviceIdType.MESH
SCALE = 2.0 / math.sqrt(D) * math.log2(math.e)
LN2 = math.log(2.0)
NT = (((1,), (1,)), ((), ()))
F32 = jnp.float32


def place():
    s = lax.axis_index("src")
    return s // 8, lax.axis_index("tgt"), (s // 2) % 4, s % 2


def device(x, y, z, c):
    return ((x * 4 + z) * 2 + c, y)


def row_peers(at):
    x, y, z, c = at
    peers = [
        (x, (y + step) % 4, z, (c + other) % 2) for step in (2, 1, 3) for other in (1, 0)
    ]
    return peers + [(x, y, z, 1 - c)]


def column_peers(at):
    x, y, z, c = at
    steps = [(a, b) for a in range(4) for b in range(4) if a or b]
    steps.sort(key=lambda t: -(min(t[0], 4 - t[0]) + min(t[1], 4 - t[1])))
    return [((x + a) % 4, y, (z + b) % 4, c) for a, b in steps]


def remote(src, dst, send, recv, to):
    return pltpu.make_async_remote_copy(
        src_ref=src,
        dst_ref=dst,
        send_sem=send,
        recv_sem=recv,
        device_id=device(*to),
        device_id_type=MESH,
    )


class Gather:
    def __init__(self, targets, planes, at, send, recv):
        self.targets, self.planes = targets, planes
        self.x, self.y, self.z, self.c = at
        self.u = self.x * (1 - self.c) + self.z * self.c
        self.v = self.z * (1 - self.c) + self.x * self.c
        self.send, self.recv = send, recv
        self.copies = {}

    def shift(self, du, dv):
        x = (self.x + du * (1 - self.c) + dv * self.c) % 4
        z = (self.z + du * self.c + dv * (1 - self.c)) % 4
        return (x, self.y, z, self.c)

    def go(self, stage, k, du, dv, low, to):
        row = ((self.u + du) % 4 * 4 + (self.v + dv) % 4) * 64 + low
        block = self.targets.at[self.planes, pl.ds(pl.multiple_of(row, 32), 32), :]
        copy = remote(block, block, self.send.at[stage, k], self.recv.at[stage, k], to)
        copy.start()
        self.copies[stage, k] = copy

    def both_ways(self, stage, du, up, down):
        self.go(stage, 0, du, 0, 0, up)
        self.go(stage, 2, du, 0, 32, down)
        self.go(stage, 1, du, 0, 32, up)
        self.go(stage, 3, du, 0, 0, down)

    def first(self):
        self.both_ways(4, 0, self.shift(1, 0), self.shift(3, 0))

    def first_forward(self):
        self.copies[4, 0].wait_recv()
        self.go(4, 4, 3, 0, 0, self.shift(1, 0))
        self.copies[4, 2].wait_recv()
        self.go(4, 5, 1, 0, 32, self.shift(3, 0))

    def second(self, du):
        if du == 3:
            self.copies[4, 1].wait_recv()
        if du == 1:
            self.copies[4, 3].wait_recv()
        if du == 2:
            self.copies[4, 4].wait_recv()
            self.copies[4, 5].wait_recv()
        self.both_ways(du, du, self.shift(0, 1), self.shift(0, 3))

    def second_forward(self, du):
        self.copies[du, 0].wait_recv()
        self.go(du, 4, du, 3, 0, self.shift(0, 1))
        self.copies[du, 2].wait_recv()
        self.go(du, 5, du, 1, 32, self.shift(0, 3))

    def arrived(self, du):
        for k in (1, 3, 4, 5):
            self.copies[du, k].wait_recv()
        return pl.multiple_of((self.u + du) % 4 * 256, 256)

    def finish(self):
        for copy in self.copies.values():
            copy.wait_send()


def combine(parts):
    peak = functools.reduce(jnp.maximum, parts)
    return peak + jnp.log2(functools.reduce(jnp.add, [jnp.exp2(p - peak) for p in parts]))


def row_pass(scores, g, out, first=0, width=8):
    lane = lax.broadcasted_iota(jnp.int32, (8, 128), 1)
    sub = lax.broadcasted_iota(jnp.int32, (8, 128), 0)
    shifts = [jnp.broadcast_to(g[k : k + 1, :], (8, 128)) for k in range(width)]

    def block(q, _):
        def group(i, acc):
            r = pl.multiple_of(q * 128 + i * 8, 8)
            xs = [
                scores[pl.ds(r, 8), pl.ds(first + 128 * k, 128)] + shifts[k] for k in range(width)
            ]
            peak = jnp.max(functools.reduce(jnp.maximum, xs), axis=1, keepdims=True)
            total = functools.reduce(jnp.add, [jnp.exp2(x - peak) for x in xs])
            value = peak + jnp.log2(jnp.sum(total, axis=1, keepdims=True))
            return jnp.where(lane - i * 8 == sub, value, acc)

        acc = lax.fori_loop(0, 16, group, jnp.zeros((8, 128), F32), unroll=16)
        out[pl.ds(q, 1), :] = jnp.sum(acc, axis=0, keepdims=True)
        return 0

    lax.fori_loop(0, 8, block, 0, unroll=2)


def spread(values, out):
    for q in range(values.shape[0]):
        out[pl.ds(q * 128, 128), :] = jnp.broadcast_to(values[q : q + 1, :], (128, 128)).T


def column_pass(scores, f_rows, out):
    def peaks(i, carry):
        r = pl.multiple_of(i * 8, 8)
        f = f_rows[pl.ds(r, 8), :]
        return tuple(
            jnp.maximum(carry[k], scores[pl.ds(r, 8), pl.ds(128 * k, 128)] + f)
            for k in range(8)
        )

    start = tuple(jnp.full((8, 128), -1e30, F32) for _ in range(8))
    top = lax.fori_loop(0, 128, peaks, start, unroll=16)
    top = [jnp.broadcast_to(jnp.max(t, axis=0, keepdims=True), (8, 128)) for t in top]

    def sums(i, carry):
        r = pl.multiple_of(i * 8, 8)
        f = f_rows[pl.ds(r, 8), :]
        return tuple(
            carry[k] + jnp.exp2(scores[pl.ds(r, 8), pl.ds(128 * k, 128)] + f - top[k])
            for k in range(8)
        )

    start = tuple(jnp.zeros((8, 128), F32) for _ in range(8))
    total = lax.fori_loop(0, 128, sums, start, unroll=16)
    for k in range(8):
        out[k : k + 1, :] = top[k][0:1] + jnp.log2(jnp.sum(total[k], axis=0, keepdims=True))


def kernel(
    source_ref, target_ref, a_ref, b_ref, readout_ref, f_ref, g_ref,
    sources, targets, masses, scores, f_rows, mass_rows, row_buf, column_buf, g_buf, order,
    weights, partial, arrived, arrived_mass,
    own_send, own_recv, far_send, far_recv, y_send, y_recv, in_send, in_recv,
    row_send, row_recv, column_send, column_recv, g_send, g_recv, out_send, out_recv,
):
    at = place()
    x, y, z, c = at
    rows, columns = row_peers(at), column_peers(at)
    barrier = pltpu.get_barrier_semaphore()
    for peer in columns + rows:
        pl.semaphore_signal(barrier, inc=1, device_id=device(*peer), device_id_type=MESH)
    pl.semaphore_wait(barrier, len(columns) + len(rows))

    sibling = (x, y, z, 1 - c)
    own = Gather(targets, pl.ds(0, 1), at, own_send, own_recv)
    far = Gather(targets, pl.ds(1, 3), at, far_send, far_recv)
    own_rows = pl.ds(pl.multiple_of((own.u * 4 + own.v) * 64, 64), 64)
    half_rows = pl.ds(pl.multiple_of(c * 512, 512), 512)
    targets[0, own_rows, :] = target_ref[...]
    own.first()
    own.second(0)
    inner = [
        remote(source_ref, sources.at[half_rows], in_send.at[0], in_recv.at[0], sibling),
        remote(a_ref, masses.at[c], in_send.at[1], in_recv.at[1], sibling),
    ]
    for copy in inner:
        copy.start()
    crossings = []
    for k, step in enumerate((1, 3, 2)):
        dst = targets.at[4 - step, own_rows]
        copy = remote(target_ref, dst, y_send.at[k], y_recv.at[k], (x, (y + step) % 4, z, c))
        copy.start()
        crossings.append(copy)
    sources[half_rows, :] = source_ref[...]
    masses[c] = a_ref[...]

    left = lax.broadcasted_iota(jnp.int32, (8, 128), 1) < 64
    for k in range(16):
        turned = k % 4 * 4 + k // 4
        order[0, k : k + 1, :] = jnp.where(
            c == 0, b_ref[k : k + 1, :], b_ref[turned : turned + 1, :]
        )
    even, odd = order[0, pl.ds(0, 8, stride=2), :], order[0, pl.ds(1, 8, stride=2), :]
    log_b = jnp.log2(
        jnp.where(
            c == 0,
            jnp.where(left, even, pltpu.roll(odd, 64, 1)),
            jnp.where(left, pltpu.roll(even, 64, 1), odd),
        )
    )

    def block_scores(plane, at_column):
        columns_at = pl.ds(at_column, 256)
        product = lax.dot_general(
            sources[...], targets[plane, columns_at, :], NT, preferred_element_type=F32
        )
        scores[plane, :, columns_at] = product * SCALE

    zeros = jnp.zeros((8, 128), F32)

    def own_block(k, du):
        column = own.arrived(du)
        block_scores(0, column)
        row_pass(scores.at[0], zeros, order.at[1 + k], column, 2)

    def far_block(du):
        column = far.arrived(du)
        for plane in (1, 2, 3):
            block_scores(plane, column)

    own.first_forward()
    own.second(3)
    own.second(1)
    own.second_forward(0)
    own.second(2)
    own.second_forward(3)
    own.second_forward(1)
    for copy in inner:
        copy.wait_recv()
    log_a = jnp.log2(jnp.concatenate([masses[0], masses[1]], axis=0))
    own_block(0, 0)
    own.second_forward(2)
    for copy in crossings:
        copy.wait_recv()
    far.first()
    far.second(0)
    own_block(1, 3)
    own_block(2, 1)
    own_block(3, 2)

    def exchange(buf, me, peers, send, recv):
        for peer in peers:
            remote(buf.at[me], buf.at[me], send, recv, peer).start()

    def drain(buf, peers, sem):
        every = buf.at[pl.ds(0, len(peers))]
        pltpu.make_async_copy(every, every, sem).wait()

    def after_row_send(it):
        if it == 0:
            far.first_forward()
        if it == 1:
            far.second_forward(0)
            far.second(2)
        if it == 2:
            far.second_forward(2)
            far_block(3)

    def after_column_send(it):
        if it == 0:
            far.second(3)
            far.second(1)
        if it == 1:
            far.second_forward(3)
            far.second_forward(1)
            far_block(0)
        if it == 2:
            far_block(1)
            far_block(2)

    g = zeros
    row_me, column_me = y * 2 + c, x * 4 + z
    for it in range(ITERS):
        if it == 0:
            row_buf[0, row_me] = combine([order[1 + k, 0:8, :] for k in range(4)])
        else:
            row_pass(scores.at[0], g, row_buf.at[it, row_me])
        exchange(row_buf.at[it], row_me, rows, row_send.at[it], row_recv.at[it])
        after_row_send(it)
        drain(row_buf.at[it], rows, row_recv.at[it])
        lse = combine([row_buf[it, k] for k in range(8)])
        f = log_a - lse
        spread(f, f_rows)
        column_pass(scores.at[0], f_rows, column_buf.at[it, column_me])
        exchange(column_buf.at[it], column_me, columns, column_send.at[it], column_recv.at[it])
        after_column_send(it)
        drain(column_buf.at[it], columns, column_recv.at[it])
        g = log_b - combine([column_buf[it, k] for k in range(16)])

    g_buf[0] = g
    shared = []
    for k, step in enumerate((2, 1, 3)):
        to = (x, (y + step) % 4, z, c)
        shared.append(remote(g_buf.at[0], g_buf.at[4 - step], g_send.at[k], g_recv.at[k], to))
    shared.append(remote(g_buf.at[0], g_buf.at[4], g_send.at[3], g_recv.at[3], sibling))
    for copy in shared:
        copy.start()

    spread(-lse, f_rows)
    mass_rows[...] = jnp.zeros_like(mass_rows)
    other = pl.multiple_of((1 - c) * 512, 512)
    mine = pl.multiple_of(c * 512, 512)

    def weigh(start, plane, slot):
        def group(i, _):
            r = pl.multiple_of(start + i * 16, 16)
            base = f_rows[pl.ds(r, 16), :]
            mass = mass_rows[pl.ds(r, 16), :]
            for q in range(8):
                shift = g_buf[plane, q : q + 1, :]
                w = jnp.exp2(scores[plane, pl.ds(r, 16), pl.ds(q * 128, 128)] + base + shift)
                mass = mass + w
                weights[slot, pl.ds(pl.multiple_of(i * 16, 16), 16), pl.ds(q * 128, 128)] = (
                    w.astype(jnp.bfloat16)
                )
            mass_rows[pl.ds(r, 16), :] = mass
            return 0

        lax.fori_loop(0, 32, group, 0, unroll=8)

    def product(plane, slot):
        return jnp.dot(weights[slot], targets[plane], preferred_element_type=F32)

    weigh(other, 0, 0)
    partial[...] = product(0, 0)
    weigh(mine, 0, 1)
    readout_ref[...] = product(0, 1)
    for copy in shared:
        copy.wait_recv()

    def other_part(plane, _):
        weigh(other, plane, 0)
        partial[...] += product(plane, 0)
        return 0

    lax.fori_loop(1, 4, other_part, 0)
    outward = [
        remote(partial, arrived, out_send.at[0], out_recv.at[0], sibling),
        remote(
            mass_rows.at[pl.ds(other, 512)], arrived_mass, out_send.at[1], out_recv.at[1], sibling
        ),
    ]
    for copy in outward:
        copy.start()

    f_ref[...] = jnp.where(c == 0, f[0:4], f[4:8]) * LN2
    here, there = g_buf[0] * LN2, g_buf[4] * LN2
    g0, g1 = jnp.where(c == 0, here, there), jnp.where(c == 0, there, here)
    order[0, pl.ds(0, 8, stride=2), :] = pltpu.roll(g1, 64, 1)
    order[0, pl.ds(1, 8, stride=2), :] = g1
    order[1, pl.ds(0, 8, stride=2), :] = g0
    order[1, pl.ds(1, 8, stride=2), :] = pltpu.roll(g0, 64, 1)
    for k in range(16):
        turned = k % 4 * 4 + k // 4
        g_ref[k : k + 1, :] = jnp.where(
            left[0:1], order[1, k : k + 1, :], order[0, turned : turned + 1, :]
        )

    def mine_part(plane, _):
        weigh(mine, plane, 1)
        readout_ref[...] += product(plane, 1)
        return 0

    lax.fori_loop(1, 4, mine_part, 0)
    for copy in outward:
        copy.wait_recv()
    mass = mass_rows[pl.ds(mine, 512), :] + arrived_mass[...]
    readout_ref[...] = (readout_ref[...] + arrived[...]) / jnp.sum(mass, axis=1, keepdims=True)

    own.finish()
    far.finish()
    for copy in inner + crossings + shared + outward:
        copy.wait_send()
    for it in range(ITERS):
        drain(row_buf.at[it], rows, row_send.at[it])
        drain(column_buf.at[it], columns, column_send.at[it])


def shards(source_embed, target_embed, source_mass, target_mass):
    vmem, dma = pltpu.VMEM, pltpu.SemaphoreType.DMA
    bf16 = jnp.bfloat16
    readout, f, g = pl.pallas_call(
        kernel,
        out_shape=(
            jax.ShapeDtypeStruct((512, D), F32),
            jax.ShapeDtypeStruct((4, 128), F32),
            jax.ShapeDtypeStruct((16, 128), F32),
        ),
        in_specs=[pl.BlockSpec(memory_space=vmem)] * 4,
        out_specs=(pl.BlockSpec(memory_space=vmem),) * 3,
        scratch_shapes=[
            vmem((1024, D), bf16),
            vmem((4, 1024, D), bf16),
            vmem((2, 4, 128), F32),
            vmem((4, 1024, 1024), F32),
            vmem((1024, 128), F32),
            vmem((1024, 128), F32),
            vmem((ITERS, 8, 8, 128), F32),
            vmem((ITERS, 16, 8, 128), F32),
            vmem((5, 8, 128), F32),
            vmem((5, 16, 128), F32),
            vmem((2, 512, 1024), bf16),
            vmem((512, D), F32),
            vmem((512, D), F32),
            vmem((512, 128), F32),
            dma((5, 6)),
            dma((5, 6)),
            dma((5, 6)),
            dma((5, 6)),
            dma((3,)),
            dma((3,)),
            dma((2,)),
            dma((2,)),
            dma((ITERS,)),
            dma((ITERS,)),
            dma((ITERS,)),
            dma((ITERS,)),
            dma((4,)),
            dma((4,)),
            dma((2,)),
            dma((2,)),
        ],
        name="sinkhorn",
        compiler_params=pltpu.CompilerParams(
            collective_id=0, has_side_effects=True, vmem_limit_bytes=56 << 20
        ),
    )(source_embed, target_embed, source_mass.reshape(4, 128), target_mass.reshape(16, 128))
    return readout, f.reshape(512), g.reshape(2048)


def solution(mesh):
    placed = (P("src", None), P(("tgt", "src"), None), P("src"), P("tgt"))
    return jax.shard_map(
        shards,
        mesh=mesh,
        in_specs=placed,
        out_specs=(P("src", None), P("src"), P("tgt")),
        check_vma=False,
    )
```

```python
import functools
import math

import jax
import jax.numpy as jnp
from jax import lax
from jax.experimental import pallas as pl
from jax.experimental.pallas import tpu as pltpu
from jax.sharding import PartitionSpec as P

D = 768
ITERS = 3
MESH = pl.DeviceIdType.MESH
SCALE = 2.0 / math.sqrt(D) * math.log2(math.e)
LN2 = math.log(2.0)
NT = (((1,), (1,)), ((), ()))
F32 = jnp.float32


def place():
    s = lax.axis_index("src")
    return s // 8, lax.axis_index("tgt"), (s // 2) % 4, s % 2


def device(x, y, z, c):
    return ((x * 4 + z) * 2 + c, y)


def row_peers(at):
    x, y, z, c = at
    peers = [
        (x, (y + step) % 4, z, (c + other) % 2) for step in (2, 1, 3) for other in (1, 0)
    ]
    return peers + [(x, y, z, 1 - c)]


def column_peers(at):
    x, y, z, c = at
    steps = [(a, b) for a in range(4) for b in range(4) if a or b]
    steps.sort(key=lambda t: -(min(t[0], 4 - t[0]) + min(t[1], 4 - t[1])))
    return [((x + a) % 4, y, (z + b) % 4, c) for a, b in steps]


def remote(src, dst, send, recv, to):
    return pltpu.make_async_remote_copy(
        src_ref=src,
        dst_ref=dst,
        send_sem=send,
        recv_sem=recv,
        device_id=device(*to),
        device_id_type=MESH,
    )


class Gather:
    def __init__(self, targets, planes, at, send, recv):
        self.targets, self.planes = targets, planes
        self.x, self.y, self.z, self.c = at
        self.u = self.x * (1 - self.c) + self.z * self.c
        self.v = self.z * (1 - self.c) + self.x * self.c
        self.send, self.recv = send, recv
        self.copies = {}

    def shift(self, du, dv):
        x = (self.x + du * (1 - self.c) + dv * self.c) % 4
        z = (self.z + du * self.c + dv * (1 - self.c)) % 4
        return (x, self.y, z, self.c)

    def go(self, stage, k, du, dv, low, to):
        row = ((self.u + du) % 4 * 4 + (self.v + dv) % 4) * 64 + low
        block = self.targets.at[self.planes, pl.ds(pl.multiple_of(row, 32), 32), :]
        copy = remote(block, block, self.send.at[stage, k], self.recv.at[stage, k], to)
        copy.start()
        self.copies[stage, k] = copy

    def both_ways(self, stage, du, up, down):
        self.go(stage, 0, du, 0, 0, up)
        self.go(stage, 2, du, 0, 32, down)
        self.go(stage, 1, du, 0, 32, up)
        self.go(stage, 3, du, 0, 0, down)

    def first(self):
        self.both_ways(4, 0, self.shift(1, 0), self.shift(3, 0))

    def first_forward(self):
        self.copies[4, 0].wait_recv()
        self.go(4, 4, 3, 0, 0, self.shift(1, 0))
        self.copies[4, 2].wait_recv()
        self.go(4, 5, 1, 0, 32, self.shift(3, 0))

    def second(self, du):
        if du == 3:
            self.copies[4, 1].wait_recv()
        if du == 1:
            self.copies[4, 3].wait_recv()
        if du == 2:
            self.copies[4, 4].wait_recv()
            self.copies[4, 5].wait_recv()
        self.both_ways(du, du, self.shift(0, 1), self.shift(0, 3))

    def second_forward(self, du):
        self.copies[du, 0].wait_recv()
        self.go(du, 4, du, 3, 0, self.shift(0, 1))
        self.copies[du, 2].wait_recv()
        self.go(du, 5, du, 1, 32, self.shift(0, 3))

    def arrived(self, du):
        for k in (1, 3, 4, 5):
            self.copies[du, k].wait_recv()
        return pl.multiple_of((self.u + du) % 4 * 256, 256)

    def finish(self):
        for copy in self.copies.values():
            copy.wait_send()


def combine(parts):
    peak = functools.reduce(jnp.maximum, parts)
    return peak + jnp.log2(functools.reduce(jnp.add, [jnp.exp2(p - peak) for p in parts]))


def row_pass(scores, g, out, first=0, width=8):
    lane = lax.broadcasted_iota(jnp.int32, (8, 128), 1)
    sub = lax.broadcasted_iota(jnp.int32, (8, 128), 0)
    shifts = [jnp.broadcast_to(g[k : k + 1, :], (8, 128)) for k in range(width)]

    def block(q, _):
        def group(i, acc):
            r = pl.multiple_of(q * 128 + i * 8, 8)
            xs = [
                scores[pl.ds(r, 8), pl.ds(first + 128 * k, 128)] + shifts[k] for k in range(width)
            ]
            peak = jnp.max(functools.reduce(jnp.maximum, xs), axis=1, keepdims=True)
            total = functools.reduce(jnp.add, [jnp.exp2(x - peak) for x in xs])
            value = peak + jnp.log2(jnp.sum(total, axis=1, keepdims=True))
            return jnp.where(lane - i * 8 == sub, value, acc)

        acc = lax.fori_loop(0, 16, group, jnp.zeros((8, 128), F32), unroll=16)
        out[pl.ds(q, 1), :] = jnp.sum(acc, axis=0, keepdims=True)
        return 0

    lax.fori_loop(0, 8, block, 0, unroll=2)


def spread(values, out):
    for q in range(values.shape[0]):
        out[pl.ds(q * 128, 128), :] = jnp.broadcast_to(values[q : q + 1, :], (128, 128)).T


def column_pass(scores, f_rows, out):
    def peaks(i, carry):
        r = pl.multiple_of(i * 8, 8)
        f = f_rows[pl.ds(r, 8), :]
        return tuple(
            jnp.maximum(carry[k], scores[pl.ds(r, 8), pl.ds(128 * k, 128)] + f)
            for k in range(8)
        )

    start = tuple(jnp.full((8, 128), -1e30, F32) for _ in range(8))
    top = lax.fori_loop(0, 128, peaks, start, unroll=16)
    top = [jnp.broadcast_to(jnp.max(t, axis=0, keepdims=True), (8, 128)) for t in top]

    def sums(i, carry):
        r = pl.multiple_of(i * 8, 8)
        f = f_rows[pl.ds(r, 8), :]
        return tuple(
            carry[k] + jnp.exp2(scores[pl.ds(r, 8), pl.ds(128 * k, 128)] + f - top[k])
            for k in range(8)
        )

    start = tuple(jnp.zeros((8, 128), F32) for _ in range(8))
    total = lax.fori_loop(0, 128, sums, start, unroll=16)
    for k in range(8):
        out[k : k + 1, :] = top[k][0:1] + jnp.log2(jnp.sum(total[k], axis=0, keepdims=True))


def kernel(
    source_ref, target_ref, a_ref, b_ref, readout_out, f_out, g_out,
    readout_ref, f_ref, g_ref,
    sources, targets, masses, b_buf, scores, f_rows, mass_rows, row_buf, column_buf, g_buf, order,
    weights_a, weights_b, partial, arrived, arrived_mass,
    load, own_send, own_recv, far_send, far_recv, y_send, y_recv, in_send, in_recv,
    row_send, row_recv, column_send, column_recv, g_send, g_recv, out_send, out_recv, store,
):
    at = place()
    x, y, z, c = at
    rows, columns = row_peers(at), column_peers(at)
    own = Gather(targets, pl.ds(0, 1), at, own_send, own_recv)
    far = Gather(targets, pl.ds(1, 3), at, far_send, far_recv)
    own_rows = pl.ds(pl.multiple_of((own.u * 4 + own.v) * 64, 64), 64)
    half_rows = pl.ds(pl.multiple_of(c * 512, 512), 512)
    own_target = targets.at[0, own_rows]
    loads = [
        pltpu.make_async_copy(target_ref, own_target, load.at[0]),
        pltpu.make_async_copy(a_ref, masses.at[c], load.at[1]),
        pltpu.make_async_copy(b_ref, b_buf, load.at[2]),
        pltpu.make_async_copy(source_ref, sources.at[half_rows], load.at[3]),
    ]
    for copy in loads:
        copy.start()
    barrier = pltpu.get_barrier_semaphore()
    for peer in columns + rows:
        pl.semaphore_signal(barrier, inc=1, device_id=device(*peer), device_id_type=MESH)
    pl.semaphore_wait(barrier, len(columns) + len(rows))

    sibling = (x, y, z, 1 - c)
    loads[0].wait()
    own.first()
    own.second(0)
    inner = [
        remote(source_ref, sources.at[half_rows], in_send.at[0], in_recv.at[0], sibling),
        remote(a_ref, masses.at[c], in_send.at[1], in_recv.at[1], sibling),
    ]
    for copy in inner:
        copy.start()
    crossings = []
    for k, step in enumerate((1, 3, 2)):
        dst = targets.at[4 - step, own_rows]
        copy = remote(own_target, dst, y_send.at[k], y_recv.at[k], (x, (y + step) % 4, z, c))
        copy.start()
        crossings.append(copy)
    for copy in loads[1:]:
        copy.wait()

    left = lax.broadcasted_iota(jnp.int32, (8, 128), 1) < 64
    for k in range(16):
        turned = k % 4 * 4 + k // 4
        order[0, k : k + 1, :] = jnp.where(
            c == 0, b_buf[k : k + 1, :], b_buf[turned : turned + 1, :]
        )
    even, odd = order[0, pl.ds(0, 8, stride=2), :], order[0, pl.ds(1, 8, stride=2), :]
    log_b = jnp.log2(
        jnp.where(
            c == 0,
            jnp.where(left, even, pltpu.roll(odd, 64, 1)),
            jnp.where(left, pltpu.roll(even, 64, 1), odd),
        )
    )

    def block_scores(plane, at_column):
        columns_at = pl.ds(at_column, 256)
        product = lax.dot_general(
            sources[...], targets[plane, columns_at, :], NT, preferred_element_type=F32
        )
        scores[plane, :, columns_at] = product * SCALE

    zeros = jnp.zeros((8, 128), F32)

    def own_block(k, du):
        column = own.arrived(du)
        block_scores(0, column)

    def far_block(du):
        column = far.arrived(du)
        for plane in (1, 2, 3):
            block_scores(plane, column)

    own.first_forward()
    own.second(3)
    own.second(1)
    own.second_forward(0)
    own.second(2)
    own.second_forward(3)
    own.second_forward(1)
    for copy in inner:
        copy.wait_recv()
    log_a = jnp.log2(jnp.concatenate([masses[0], masses[1]], axis=0))
    own_block(0, 0)
    own.second_forward(2)
    for copy in crossings:
        copy.wait_recv()
    far.first()
    far.second(0)
    own_block(1, 3)
    own_block(2, 1)
    own_block(3, 2)

    def exchange(buf, me, peers, send, recv):
        for peer in peers:
            remote(buf.at[me], buf.at[me], send, recv, peer).start()

    def drain(buf, peers, sem):
        every = buf.at[pl.ds(0, len(peers))]
        pltpu.make_async_copy(every, every, sem).wait()

    def after_row_send(it):
        if it == 0:
            far.first_forward()
        if it == 1:
            far.second_forward(0)
            far.second(2)
        if it == 2:
            far.second_forward(2)
            far_block(3)

    def after_column_send(it):
        if it == 0:
            far.second(3)
            far.second(1)
        if it == 1:
            far.second_forward(3)
            far.second_forward(1)
            far_block(0)
        if it == 2:
            far_block(1)
            far_block(2)

    g = zeros
    row_me, column_me = y * 2 + c, x * 4 + z
    for it in range(ITERS):
        row_pass(scores.at[0], g, row_buf.at[it, row_me])
        exchange(row_buf.at[it], row_me, rows, row_send.at[it], row_recv.at[it])
        after_row_send(it)
        drain(row_buf.at[it], rows, row_recv.at[it])
        lse = combine([row_buf[it, k] for k in range(8)])
        f = log_a - lse
        spread(f, f_rows)
        column_pass(scores.at[0], f_rows, column_buf.at[it, column_me])
        exchange(column_buf.at[it], column_me, columns, column_send.at[it], column_recv.at[it])
        after_column_send(it)
        drain(column_buf.at[it], columns, column_recv.at[it])
        g = log_b - combine([column_buf[it, k] for k in range(16)])

    g_buf[0] = g
    shared = []
    for k, step in enumerate((2, 1, 3)):
        to = (x, (y + step) % 4, z, c)
        shared.append(remote(g_buf.at[0], g_buf.at[4 - step], g_send.at[k], g_recv.at[k], to))
    shared.append(remote(g_buf.at[0], g_buf.at[4], g_send.at[3], g_recv.at[3], sibling))
    for copy in shared:
        copy.start()

    spread(-lse, f_rows)
    other = pl.multiple_of((1 - c) * 512, 512)
    mine = pl.multiple_of(c * 512, 512)

    def weigh(start, plane, low):
        shifts = [g_buf[plane, q : q + 1, :] for q in range(8)]
        for i in range(32):
            r = pl.multiple_of(start + i * 16, 16)
            base = f_rows[pl.ds(r, 16), :]
            parts = [
                jnp.exp2(scores[plane, pl.ds(r, 16), q * 128 : (q + 1) * 128] + base + shifts[q])
                for q in range(8)
            ]
            mass = functools.reduce(jnp.add, parts)
            if plane:
                mass = mass + mass_rows[pl.ds(r, 16), :]
            mass_rows[pl.ds(r, 16), :] = mass
            for q in range(8):
                low[i * 16 : (i + 1) * 16, q * 128 : (q + 1) * 128] = parts[q].astype(jnp.bfloat16)

    def product(plane, low, out):
        value = jnp.dot(low[...], targets[plane], preferred_element_type=F32)
        out[...] = out[...] + value if plane else value

    weigh(other, 0, weights_a)
    product(0, weights_a, partial)
    weigh(mine, 0, weights_b)
    for copy in shared:
        copy.wait_recv()
    product(0, weights_b, readout_ref)
    weigh(other, 1, weights_a)
    product(1, weights_a, partial)
    weigh(other, 2, weights_b)
    product(2, weights_b, partial)
    weigh(other, 3, weights_a)
    product(3, weights_a, partial)
    outward = [
        remote(partial, arrived, out_send.at[0], out_recv.at[0], sibling),
        remote(
            mass_rows.at[pl.ds(other, 512)], arrived_mass, out_send.at[1], out_recv.at[1], sibling
        ),
    ]
    for copy in outward:
        copy.start()

    f_ref[...] = jnp.where(c == 0, f[0:4], f[4:8]) * LN2
    here, there = g_buf[0] * LN2, g_buf[4] * LN2
    g0, g1 = jnp.where(c == 0, here, there), jnp.where(c == 0, there, here)
    order[0, pl.ds(0, 8, stride=2), :] = pltpu.roll(g1, 64, 1)
    order[0, pl.ds(1, 8, stride=2), :] = g1
    order[1, pl.ds(0, 8, stride=2), :] = g0
    order[1, pl.ds(1, 8, stride=2), :] = pltpu.roll(g0, 64, 1)
    for k in range(16):
        turned = k % 4 * 4 + k // 4
        g_ref[k : k + 1, :] = jnp.where(
            left[0:1], order[1, k : k + 1, :], order[0, turned : turned + 1, :]
        )

    weigh(mine, 1, weights_b)
    product(1, weights_b, readout_ref)
    weigh(mine, 2, weights_a)
    product(2, weights_a, readout_ref)
    weigh(mine, 3, weights_b)
    product(3, weights_b, readout_ref)
    for copy in outward:
        copy.wait_recv()
    stores = [
        pltpu.make_async_copy(f_ref, f_out, store.at[4]),
        pltpu.make_async_copy(g_ref, g_out, store.at[5]),
    ]
    for copy in stores:
        copy.start()
    for k in range(4):
        part = pl.ds(k * 128, 128)
        mass = mass_rows[pl.ds(pl.multiple_of(mine + k * 128, 128), 128), :] + arrived_mass[part, :]
        readout_ref[part, :] = (readout_ref[part, :] + arrived[part, :]) * (
            1.0 / jnp.sum(mass, axis=1, keepdims=True)
        )
        copy = pltpu.make_async_copy(readout_ref.at[part], readout_out.at[part], store.at[k])
        copy.start()
        stores.append(copy)

    own.finish()
    far.finish()
    for copy in inner + crossings + shared + outward:
        copy.wait_send()
    for it in range(ITERS):
        drain(row_buf.at[it], rows, row_send.at[it])
        drain(column_buf.at[it], columns, column_send.at[it])
    for copy in stores:
        copy.wait()


def finish(readout, f, g, readout_out, f_out, g_out, held, held_f, held_g, load, store):
    pairs = [(f, held_f, f_out), (g, held_g, g_out)]
    for k in range(8):
        part = pl.ds(k * 64, 64)
        pairs.append((readout.at[part], held.at[part], readout_out.at[part]))
    loads = [pltpu.make_async_copy(a, b, load.at[k]) for k, (a, b, _) in enumerate(pairs)]
    stores = [pltpu.make_async_copy(b, o, store.at[k]) for k, (_, b, o) in enumerate(pairs)]
    for copy in loads:
        copy.start()
    for before, after in zip(loads, stores):
        before.wait()
        after.start()
    for copy in stores:
        copy.wait()


def shards(source_embed, target_embed, source_mass, target_mass):
    vmem, dma = pltpu.VMEM, pltpu.SemaphoreType.DMA
    bf16 = jnp.bfloat16
    readout, f, g = pl.pallas_call(
        kernel,
        out_shape=(
            jax.ShapeDtypeStruct((512, D), F32),
            jax.ShapeDtypeStruct((4, 128), F32),
            jax.ShapeDtypeStruct((16, 128), F32),
        ),
        in_specs=[pl.BlockSpec(memory_space=pltpu.HBM)] * 4,
        out_specs=(pl.BlockSpec(memory_space=pltpu.HBM),) * 3,
        scratch_shapes=[
            vmem((512, D), F32),
            vmem((4, 128), F32),
            vmem((16, 128), F32),
            vmem((1024, D), bf16),
            vmem((4, 1024, D), bf16),
            vmem((2, 4, 128), F32),
            vmem((16, 128), F32),
            vmem((4, 1024, 1024), F32),
            vmem((1024, 128), F32),
            vmem((1024, 128), F32),
            vmem((ITERS, 8, 8, 128), F32),
            vmem((ITERS, 16, 8, 128), F32),
            vmem((5, 8, 128), F32),
            vmem((5, 16, 128), F32),
            vmem((512, 1024), bf16),
            vmem((512, 1024), bf16),
            vmem((512, D), F32),
            vmem((512, D), F32),
            vmem((512, 128), F32),
            dma((4,)),
            dma((5, 6)),
            dma((5, 6)),
            dma((5, 6)),
            dma((5, 6)),
            dma((3,)),
            dma((3,)),
            dma((2,)),
            dma((2,)),
            dma((ITERS,)),
            dma((ITERS,)),
            dma((ITERS,)),
            dma((ITERS,)),
            dma((4,)),
            dma((4,)),
            dma((2,)),
            dma((2,)),
            dma((6,)),
        ],
        name="sinkhorn",
        compiler_params=pltpu.CompilerParams(
            collective_id=0, has_side_effects=True, vmem_limit_bytes=56 << 20
        ),
    )(source_embed, target_embed, source_mass.reshape(4, 128), target_mass.reshape(16, 128))
    readout, f, g = pl.pallas_call(
        finish,
        out_shape=(
            jax.ShapeDtypeStruct((512, D), F32),
            jax.ShapeDtypeStruct((4, 128), F32),
            jax.ShapeDtypeStruct((16, 128), F32),
        ),
        in_specs=[pl.BlockSpec(memory_space=pl.ANY)] * 3,
        out_specs=(pl.BlockSpec(memory_space=pl.ANY),) * 3,
        scratch_shapes=[
            vmem((512, D), F32),
            vmem((4, 128), F32),
            vmem((16, 128), F32),
            dma((10,)),
            dma((10,)),
        ],
        name="finish",
        compiler_params=pltpu.CompilerParams(vmem_limit_bytes=60 << 20),
    )(readout, f, g)
    return readout, f.reshape(512), g.reshape(2048)


def solution(mesh):
    placed = (P("src", None), P(("tgt", "src"), None), P("src"), P("tgt"))
    return jax.shard_map(
        shards,
        mesh=mesh,
        in_specs=placed,
        out_specs=(P("src", None), P("src"), P("tgt")),
        check_vma=False,
    )
```

```python
import functools
import math

import jax
import jax.numpy as jnp
from jax import lax
from jax.experimental import pallas as pl
from jax.experimental.pallas import tpu as pltpu
from jax.sharding import PartitionSpec as P

D = 768
ITERS = 3
MESH = pl.DeviceIdType.MESH
SCALE = 2.0 / math.sqrt(D) * math.log2(math.e)
LN2 = math.log(2.0)
NT = (((1,), (1,)), ((), ()))
F32 = jnp.float32


def place():
    s = lax.axis_index("src")
    return s // 8, lax.axis_index("tgt"), (s // 2) % 4, s % 2


def device(x, y, z, c):
    return ((x * 4 + z) * 2 + c, y)


def row_peers(at):
    x, y, z, c = at
    peers = [
        (x, (y + step) % 4, z, (c + other) % 2) for step in (2, 1, 3) for other in (1, 0)
    ]
    return peers + [(x, y, z, 1 - c)]


def column_peers(at):
    x, y, z, c = at
    steps = [(a, b) for a in range(4) for b in range(4) if a or b]
    steps.sort(key=lambda t: -(min(t[0], 4 - t[0]) + min(t[1], 4 - t[1])))
    return [((x + a) % 4, y, (z + b) % 4, c) for a, b in steps]


def remote(src, dst, send, recv, to):
    return pltpu.make_async_remote_copy(
        src_ref=src,
        dst_ref=dst,
        send_sem=send,
        recv_sem=recv,
        device_id=device(*to),
        device_id_type=MESH,
    )


class Gather:
    def __init__(self, targets, planes, at, send, recv):
        self.targets, self.planes = targets, planes
        self.x, self.y, self.z, self.c = at
        self.u = self.x * (1 - self.c) + self.z * self.c
        self.v = self.z * (1 - self.c) + self.x * self.c
        self.send, self.recv = send, recv
        self.copies = {}

    def shift(self, du, dv):
        x = (self.x + du * (1 - self.c) + dv * self.c) % 4
        z = (self.z + du * self.c + dv * (1 - self.c)) % 4
        return (x, self.y, z, self.c)

    def go(self, stage, k, du, dv, low, to):
        row = ((self.u + du) % 4 * 4 + (self.v + dv) % 4) * 64 + low
        block = self.targets.at[self.planes, pl.ds(pl.multiple_of(row, 32), 32), :]
        copy = remote(block, block, self.send.at[stage, k], self.recv.at[stage, k], to)
        copy.start()
        self.copies[stage, k] = copy

    def both_ways(self, stage, du, up, down):
        self.go(stage, 0, du, 0, 0, up)
        self.go(stage, 2, du, 0, 32, down)
        self.go(stage, 1, du, 0, 32, up)
        self.go(stage, 3, du, 0, 0, down)

    def first(self):
        self.both_ways(4, 0, self.shift(1, 0), self.shift(3, 0))

    def first_forward(self):
        self.copies[4, 0].wait_recv()
        self.go(4, 4, 3, 0, 0, self.shift(1, 0))
        self.copies[4, 2].wait_recv()
        self.go(4, 5, 1, 0, 32, self.shift(3, 0))

    def second(self, du):
        if du == 3:
            self.copies[4, 1].wait_recv()
        if du == 1:
            self.copies[4, 3].wait_recv()
        if du == 2:
            self.copies[4, 4].wait_recv()
            self.copies[4, 5].wait_recv()
        self.both_ways(du, du, self.shift(0, 1), self.shift(0, 3))

    def second_forward(self, du):
        self.copies[du, 0].wait_recv()
        self.go(du, 4, du, 3, 0, self.shift(0, 1))
        self.copies[du, 2].wait_recv()
        self.go(du, 5, du, 1, 32, self.shift(0, 3))

    def arrived(self, du):
        for k in (1, 3, 4, 5):
            self.copies[du, k].wait_recv()
        return pl.multiple_of((self.u + du) % 4 * 256, 256)

    def finish(self):
        for copy in self.copies.values():
            copy.wait_send()


def combine(parts):
    peak = functools.reduce(jnp.maximum, parts)
    return peak + jnp.log2(functools.reduce(jnp.add, [jnp.exp2(p - peak) for p in parts]))


def row_pass(scores, g, half, out):
    lane = lax.broadcasted_iota(jnp.int32, (8, 128), 1)
    sub = lax.broadcasted_iota(jnp.int32, (8, 128), 0)
    shifts = [jnp.broadcast_to(g[k : k + 1, :], (8, 128)) for k in range(8)]

    def block(q, _):
        def group(i, acc):
            r = pl.multiple_of(half * 512 + q * 128 + i * 8, 8)
            xs = [scores[pl.ds(r, 8), pl.ds(128 * k, 128)] + shifts[k] for k in range(8)]
            peak = jnp.max(functools.reduce(jnp.maximum, xs), axis=1, keepdims=True)
            total = functools.reduce(jnp.add, [jnp.exp2(x - peak) for x in xs])
            value = peak + jnp.log2(jnp.sum(total, axis=1, keepdims=True))
            return jnp.where(lane - i * 8 == sub, value, acc)

        acc = lax.fori_loop(0, 16, group, jnp.zeros((8, 128), F32), unroll=16)
        out[pl.ds(q, 1), :] = jnp.sum(acc, axis=0, keepdims=True)
        return 0

    lax.fori_loop(0, 4, block, 0, unroll=2)


def spread(values, out, first=0):
    for q in range(values.shape[0]):
        rows = pl.ds(first + q * 128, 128)
        out[rows, :] = jnp.broadcast_to(values[q : q + 1, :], (128, 128)).T


def column_half(scores, f_rows, half):
    def peaks(i, carry):
        r = pl.multiple_of(half * 512 + i * 8, 8)
        f = f_rows[pl.ds(r, 8), :]
        return tuple(
            jnp.maximum(carry[k], scores[pl.ds(r, 8), pl.ds(128 * k, 128)] + f)
            for k in range(8)
        )

    start = tuple(jnp.full((8, 128), -1e30, F32) for _ in range(8))
    top = lax.fori_loop(0, 64, peaks, start, unroll=16)
    top = [jnp.broadcast_to(jnp.max(t, axis=0, keepdims=True), (8, 128)) for t in top]

    def sums(i, carry):
        r = pl.multiple_of(half * 512 + i * 8, 8)
        f = f_rows[pl.ds(r, 8), :]
        return tuple(
            carry[k] + jnp.exp2(scores[pl.ds(r, 8), pl.ds(128 * k, 128)] + f - top[k])
            for k in range(8)
        )

    start = tuple(jnp.zeros((8, 128), F32) for _ in range(8))
    return top, lax.fori_loop(0, 64, sums, start, unroll=16)


def join_columns(first, second, out):
    for k in range(8):
        peak = jnp.maximum(first[0][k], second[0][k])
        total = first[1][k] * jnp.exp2(first[0][k] - peak)
        total = total + second[1][k] * jnp.exp2(second[0][k] - peak)
        out[k : k + 1, :] = peak[0:1] + jnp.log2(jnp.sum(total, axis=0, keepdims=True))


def kernel(
    source_ref, target_ref, a_ref, b_ref, readout_out, f_out, g_out,
    readout_ref, f_ref, g_ref,
    sources, targets, masses, b_buf, scores, f_rows, mass_rows, row_buf, column_buf, g_buf, order,
    weights_a, weights_b, partial, arrived, arrived_mass,
    load, own_send, own_recv, far_send, far_recv, y_send, y_recv, in_send, in_recv,
    row_send, row_recv, column_send, column_recv, g_send, g_recv, out_send, out_recv, store,
):
    at = place()
    x, y, z, c = at
    rows, columns = row_peers(at), column_peers(at)
    own = Gather(targets, pl.ds(0, 1), at, own_send, own_recv)
    far = Gather(targets, pl.ds(1, 3), at, far_send, far_recv)
    own_rows = pl.ds(pl.multiple_of((own.u * 4 + own.v) * 64, 64), 64)
    half_rows = pl.ds(pl.multiple_of(c * 512, 512), 512)
    own_target = targets.at[0, own_rows]
    loads = [
        pltpu.make_async_copy(target_ref, own_target, load.at[0]),
        pltpu.make_async_copy(a_ref, masses.at[c], load.at[1]),
        pltpu.make_async_copy(b_ref, b_buf, load.at[2]),
        pltpu.make_async_copy(source_ref, sources.at[half_rows], load.at[3]),
    ]
    for copy in loads:
        copy.start()
    barrier = pltpu.get_barrier_semaphore()
    for peer in columns + rows:
        pl.semaphore_signal(barrier, inc=1, device_id=device(*peer), device_id_type=MESH)
    pl.semaphore_wait(barrier, len(columns) + len(rows))

    sibling = (x, y, z, 1 - c)
    loads[0].wait()
    own.first()
    own.second(0)
    inner = [
        remote(source_ref, sources.at[half_rows], in_send.at[0], in_recv.at[0], sibling),
        remote(a_ref, masses.at[c], in_send.at[1], in_recv.at[1], sibling),
    ]
    for copy in inner:
        copy.start()
    crossings = []
    for k, step in enumerate((1, 3, 2)):
        dst = targets.at[4 - step, own_rows]
        copy = remote(own_target, dst, y_send.at[k], y_recv.at[k], (x, (y + step) % 4, z, c))
        copy.start()
        crossings.append(copy)
    for copy in loads[1:]:
        copy.wait()

    left = lax.broadcasted_iota(jnp.int32, (8, 128), 1) < 64
    for k in range(16):
        turned = k % 4 * 4 + k // 4
        order[0, k : k + 1, :] = jnp.where(
            c == 0, b_buf[k : k + 1, :], b_buf[turned : turned + 1, :]
        )
    even, odd = order[0, pl.ds(0, 8, stride=2), :], order[0, pl.ds(1, 8, stride=2), :]
    log_b = jnp.log2(
        jnp.where(
            c == 0,
            jnp.where(left, even, pltpu.roll(odd, 64, 1)),
            jnp.where(left, pltpu.roll(even, 64, 1), odd),
        )
    )

    def block_scores(plane, at_column):
        columns_at = pl.ds(at_column, 256)
        product = lax.dot_general(
            sources[...], targets[plane, columns_at, :], NT, preferred_element_type=F32
        )
        scores[plane, :, columns_at] = product * SCALE

    zeros = jnp.zeros((8, 128), F32)

    def own_block(k, du):
        column = own.arrived(du)
        block_scores(0, column)

    def far_block(du):
        column = far.arrived(du)

        def one(plane, _):
            block_scores(plane, column)
            return 0

        lax.fori_loop(1, 4, one, 0)

    own.first_forward()
    own.second(3)
    own.second(1)
    own.second_forward(0)
    own.second(2)
    own.second_forward(3)
    own.second_forward(1)
    for copy in inner:
        copy.wait_recv()
    log_a = jnp.log2(jnp.concatenate([masses[0], masses[1]], axis=0))
    own_block(0, 0)
    own.second_forward(2)
    for copy in crossings:
        copy.wait_recv()
    far.first()
    far.second(0)
    own_block(1, 3)
    own_block(2, 1)
    own_block(3, 2)

    def exchange(buf, me, peers, send, recv):
        for peer in peers:
            remote(buf.at[me], buf.at[me], send, recv, peer).start()

    def drain(buf, peers, sem):
        every = buf.at[pl.ds(0, len(peers))]
        pltpu.make_async_copy(every, every, sem).wait()

    def after_row_send(it):
        if it == 0:
            far.first_forward()
        if it == 1:
            far.second_forward(0)
            far.second(2)
        if it == 2:
            far.second_forward(2)
            far_block(3)

    def after_column_send(it):
        if it == 0:
            far.second(3)
            far.second(1)
        if it == 1:
            far.second_forward(3)
            far.second_forward(1)
            far_block(0)
        if it == 2:
            far_block(1)
            far_block(2)

    g = zeros
    row_me, column_me = y * 2 + c, x * 4 + z
    for it in range(ITERS):
        for h in (0, 1):
            row_pass(scores.at[0], g, h, row_buf.at[it, h, row_me])
            exchange(row_buf.at[it, h], row_me, rows, row_send.at[it, h], row_recv.at[it, h])
        after_row_send(it)
        halves, lses, fs = [], [], []
        for h in (0, 1):
            drain(row_buf.at[it, h], rows, row_recv.at[it, h])
            lses.append(combine([row_buf[it, h, k] for k in range(8)]))
            fs.append(log_a[h * 4 : h * 4 + 4] - lses[h])
            spread(fs[h], f_rows, h * 512)
            halves.append(column_half(scores.at[0], f_rows, h))
        lse, f = jnp.concatenate(lses, axis=0), jnp.concatenate(fs, axis=0)
        join_columns(*halves, column_buf.at[it, column_me])
        exchange(column_buf.at[it], column_me, columns, column_send.at[it], column_recv.at[it])
        after_column_send(it)
        drain(column_buf.at[it], columns, column_recv.at[it])
        g = log_b - combine([column_buf[it, k] for k in range(16)])

    g_buf[0] = g
    shared = []
    for k, step in enumerate((2, 1, 3)):
        to = (x, (y + step) % 4, z, c)
        shared.append(remote(g_buf.at[0], g_buf.at[4 - step], g_send.at[k], g_recv.at[k], to))
    shared.append(remote(g_buf.at[0], g_buf.at[4], g_send.at[3], g_recv.at[3], sibling))
    for copy in shared:
        copy.start()

    spread(-lse, f_rows)
    other = pl.multiple_of((1 - c) * 512, 512)
    mine = pl.multiple_of(c * 512, 512)

    def weigh(start, plane, low):
        shifts = [g_buf[plane, q : q + 1, :] for q in range(8)]
        for i in range(32):
            r = pl.multiple_of(start + i * 16, 16)
            base = f_rows[pl.ds(r, 16), :]
            parts = [
                jnp.exp2(scores[plane, pl.ds(r, 16), q * 128 : (q + 1) * 128] + base + shifts[q])
                for q in range(8)
            ]
            mass = functools.reduce(jnp.add, parts)
            if plane:
                mass = mass + mass_rows[pl.ds(r, 16), :]
            mass_rows[pl.ds(r, 16), :] = mass
            for q in range(8):
                low[i * 16 : (i + 1) * 16, q * 128 : (q + 1) * 128] = parts[q].astype(jnp.bfloat16)

    def product(plane, low, out):
        value = jnp.dot(low[...], targets[plane], preferred_element_type=F32)
        out[...] = out[...] + value if plane else value

    weigh(other, 0, weights_a)
    product(0, weights_a, partial)
    weigh(mine, 0, weights_b)
    for copy in shared:
        copy.wait_recv()
    product(0, weights_b, readout_ref)
    weigh(other, 1, weights_a)
    product(1, weights_a, partial)
    weigh(other, 2, weights_b)
    product(2, weights_b, partial)
    weigh(other, 3, weights_a)
    product(3, weights_a, partial)
    outward = [
        remote(partial, arrived, out_send.at[0], out_recv.at[0], sibling),
        remote(
            mass_rows.at[pl.ds(other, 512)], arrived_mass, out_send.at[1], out_recv.at[1], sibling
        ),
    ]
    for copy in outward:
        copy.start()

    f_ref[...] = jnp.where(c == 0, f[0:4], f[4:8]) * LN2
    here, there = g_buf[0] * LN2, g_buf[4] * LN2
    g0, g1 = jnp.where(c == 0, here, there), jnp.where(c == 0, there, here)
    order[0, pl.ds(0, 8, stride=2), :] = pltpu.roll(g1, 64, 1)
    order[0, pl.ds(1, 8, stride=2), :] = g1
    order[1, pl.ds(0, 8, stride=2), :] = g0
    order[1, pl.ds(1, 8, stride=2), :] = pltpu.roll(g0, 64, 1)
    for k in range(16):
        turned = k % 4 * 4 + k // 4
        g_ref[k : k + 1, :] = jnp.where(
            left[0:1], order[1, k : k + 1, :], order[0, turned : turned + 1, :]
        )

    weigh(mine, 1, weights_b)
    product(1, weights_b, readout_ref)
    weigh(mine, 2, weights_a)
    product(2, weights_a, readout_ref)
    weigh(mine, 3, weights_b)
    product(3, weights_b, readout_ref)
    for copy in outward:
        copy.wait_recv()
    stores = [
        pltpu.make_async_copy(f_ref, f_out, store.at[4]),
        pltpu.make_async_copy(g_ref, g_out, store.at[5]),
    ]
    for copy in stores:
        copy.start()
    for k in range(4):
        part = pl.ds(k * 128, 128)
        mass = mass_rows[pl.ds(pl.multiple_of(mine + k * 128, 128), 128), :] + arrived_mass[part, :]
        readout_ref[part, :] = (readout_ref[part, :] + arrived[part, :]) * (
            1.0 / jnp.sum(mass, axis=1, keepdims=True)
        )
        copy = pltpu.make_async_copy(readout_ref.at[part], readout_out.at[part], store.at[k])
        copy.start()
        stores.append(copy)

    own.finish()
    far.finish()
    for copy in inner + crossings + shared + outward:
        copy.wait_send()
    for it in range(ITERS):
        for h in (0, 1):
            drain(row_buf.at[it, h], rows, row_send.at[it, h])
        drain(column_buf.at[it], columns, column_send.at[it])
    for copy in stores:
        copy.wait()


def finish(readout, f, g, readout_out, f_out, g_out, held, held_f, held_g, load, store):
    pairs = [(f, held_f, f_out), (g, held_g, g_out)]
    for k in range(8):
        part = pl.ds(k * 64, 64)
        pairs.append((readout.at[part], held.at[part], readout_out.at[part]))
    loads = [pltpu.make_async_copy(a, b, load.at[k]) for k, (a, b, _) in enumerate(pairs)]
    stores = [pltpu.make_async_copy(b, o, store.at[k]) for k, (_, b, o) in enumerate(pairs)]
    for copy in loads:
        copy.start()
    for before, after in zip(loads, stores):
        before.wait()
        after.start()
    for copy in stores:
        copy.wait()


def shards(source_embed, target_embed, source_mass, target_mass):
    vmem, dma = pltpu.VMEM, pltpu.SemaphoreType.DMA
    bf16 = jnp.bfloat16
    readout, f, g = pl.pallas_call(
        kernel,
        out_shape=(
            jax.ShapeDtypeStruct((512, D), F32),
            jax.ShapeDtypeStruct((4, 128), F32),
            jax.ShapeDtypeStruct((16, 128), F32),
        ),
        in_specs=[pl.BlockSpec(memory_space=pltpu.HBM)] * 4,
        out_specs=(pl.BlockSpec(memory_space=pltpu.HBM),) * 3,
        scratch_shapes=[
            vmem((512, D), F32),
            vmem((4, 128), F32),
            vmem((16, 128), F32),
            vmem((1024, D), bf16),
            vmem((4, 1024, D), bf16),
            vmem((2, 4, 128), F32),
            vmem((16, 128), F32),
            vmem((4, 1024, 1024), F32),
            vmem((1024, 128), F32),
            vmem((1024, 128), F32),
            vmem((ITERS, 2, 8, 4, 128), F32),
            vmem((ITERS, 16, 8, 128), F32),
            vmem((5, 8, 128), F32),
            vmem((5, 16, 128), F32),
            vmem((512, 1024), bf16),
            vmem((512, 1024), bf16),
            vmem((512, D), F32),
            vmem((512, D), F32),
            vmem((512, 128), F32),
            dma((4,)),
            dma((5, 6)),
            dma((5, 6)),
            dma((5, 6)),
            dma((5, 6)),
            dma((3,)),
            dma((3,)),
            dma((2,)),
            dma((2,)),
            dma((ITERS, 2)),
            dma((ITERS, 2)),
            dma((ITERS,)),
            dma((ITERS,)),
            dma((4,)),
            dma((4,)),
            dma((2,)),
            dma((2,)),
            dma((6,)),
        ],
        name="sinkhorn",
        compiler_params=pltpu.CompilerParams(
            collective_id=0, has_side_effects=True, vmem_limit_bytes=56 << 20
        ),
    )(source_embed, target_embed, source_mass.reshape(4, 128), target_mass.reshape(16, 128))
    readout, f, g = pl.pallas_call(
        finish,
        out_shape=(
            jax.ShapeDtypeStruct((512, D), F32),
            jax.ShapeDtypeStruct((4, 128), F32),
            jax.ShapeDtypeStruct((16, 128), F32),
        ),
        in_specs=[pl.BlockSpec(memory_space=pl.ANY)] * 3,
        out_specs=(pl.BlockSpec(memory_space=pl.ANY),) * 3,
        scratch_shapes=[
            vmem((512, D), F32),
            vmem((4, 128), F32),
            vmem((16, 128), F32),
            dma((10,)),
            dma((10,)),
        ],
        name="finish",
        compiler_params=pltpu.CompilerParams(vmem_limit_bytes=60 << 20),
    )(readout, f, g)
    return readout, f.reshape(512), g.reshape(2048)


def solution(mesh):
    placed = (P("src", None), P(("tgt", "src"), None), P("src"), P("tgt"))
    return jax.shard_map(
        shards,
        mesh=mesh,
        in_specs=placed,
        out_specs=(P("src", None), P("src"), P("tgt")),
        check_vma=False,
    )
```

```python
import functools
import math

import jax
import jax.numpy as jnp
from jax import lax
from jax.experimental import pallas as pl
from jax.experimental.pallas import tpu as pltpu
from jax.sharding import PartitionSpec as P

D = 768
ITERS = 3
MESH = pl.DeviceIdType.MESH
SCALE = 2.0 / math.sqrt(D) * math.log2(math.e)
LN2 = math.log(2.0)
NT = (((1,), (1,)), ((), ()))
F32 = jnp.float32


def place():
    s = lax.axis_index("src")
    return s // 8, lax.axis_index("tgt"), (s // 2) % 4, s % 2


def device(x, y, z, c):
    return ((x * 4 + z) * 2 + c, y)


def row_peers(at):
    x, y, z, c = at
    peers = [
        (x, (y + step) % 4, z, (c + other) % 2) for step in (2, 1, 3) for other in (1, 0)
    ]
    return peers + [(x, y, z, 1 - c)]


def column_peers(at):
    x, y, z, c = at
    steps = [(a, b) for a in range(4) for b in range(4) if a or b]
    steps.sort(key=lambda t: -(min(t[0], 4 - t[0]) + min(t[1], 4 - t[1])))
    return [((x + a) % 4, y, (z + b) % 4, c) for a, b in steps]


def remote(src, dst, send, recv, to):
    return pltpu.make_async_remote_copy(
        src_ref=src,
        dst_ref=dst,
        send_sem=send,
        recv_sem=recv,
        device_id=device(*to),
        device_id_type=MESH,
    )


class Gather:
    def __init__(self, targets, planes, at, send, recv):
        self.targets, self.planes = targets, planes
        self.x, self.y, self.z, self.c = at
        self.u = self.x * (1 - self.c) + self.z * self.c
        self.v = self.z * (1 - self.c) + self.x * self.c
        self.send, self.recv = send, recv
        self.copies = {}

    def shift(self, du, dv):
        x = (self.x + du * (1 - self.c) + dv * self.c) % 4
        z = (self.z + du * self.c + dv * (1 - self.c)) % 4
        return (x, self.y, z, self.c)

    def go(self, stage, k, du, dv, low, to):
        row = ((self.u + du) % 4 * 4 + (self.v + dv) % 4) * 64 + low
        block = self.targets.at[self.planes, pl.ds(pl.multiple_of(row, 32), 32), :]
        copy = remote(block, block, self.send.at[stage, k], self.recv.at[stage, k], to)
        copy.start()
        self.copies[stage, k] = copy

    def both_ways(self, stage, du, up, down):
        self.go(stage, 0, du, 0, 0, up)
        self.go(stage, 2, du, 0, 32, down)
        self.go(stage, 1, du, 0, 32, up)
        self.go(stage, 3, du, 0, 0, down)

    def first(self):
        self.both_ways(4, 0, self.shift(1, 0), self.shift(3, 0))

    def first_forward(self):
        self.copies[4, 0].wait_recv()
        self.go(4, 4, 3, 0, 0, self.shift(1, 0))
        self.copies[4, 2].wait_recv()
        self.go(4, 5, 1, 0, 32, self.shift(3, 0))

    def second(self, du):
        if du == 3:
            self.copies[4, 1].wait_recv()
        if du == 1:
            self.copies[4, 3].wait_recv()
        if du == 2:
            self.copies[4, 4].wait_recv()
            self.copies[4, 5].wait_recv()
        self.both_ways(du, du, self.shift(0, 1), self.shift(0, 3))

    def second_forward(self, du):
        self.copies[du, 0].wait_recv()
        self.go(du, 4, du, 3, 0, self.shift(0, 1))
        self.copies[du, 2].wait_recv()
        self.go(du, 5, du, 1, 32, self.shift(0, 3))

    def arrived(self, du):
        for k in (1, 3, 4, 5):
            self.copies[du, k].wait_recv()
        return pl.multiple_of((self.u + du) % 4 * 256, 256)

    def finish(self):
        for copy in self.copies.values():
            copy.wait_send()


def combine(parts):
    peak = functools.reduce(jnp.maximum, parts)
    return peak + jnp.log2(functools.reduce(jnp.add, [jnp.exp2(p - peak) for p in parts]))


def row_pass(scores, g, half, out):
    lane = lax.broadcasted_iota(jnp.int32, (8, 128), 1)
    sub = lax.broadcasted_iota(jnp.int32, (8, 128), 0)
    shifts = [jnp.broadcast_to(g[k : k + 1, :], (8, 128)) for k in range(8)]

    def block(q, _):
        def group(i, acc):
            r = pl.multiple_of(half * 512 + q * 128 + i * 8, 8)
            xs = [scores[pl.ds(r, 8), pl.ds(128 * k, 128)] + shifts[k] for k in range(8)]
            peak = jnp.max(functools.reduce(jnp.maximum, xs), axis=1, keepdims=True)
            total = functools.reduce(jnp.add, [jnp.exp2(x - peak) for x in xs])
            value = peak + jnp.log2(jnp.sum(total, axis=1, keepdims=True))
            return jnp.where(lane - i * 8 == sub, value, acc)

        acc = lax.fori_loop(0, 16, group, jnp.zeros((8, 128), F32), unroll=16)
        out[pl.ds(q, 1), :] = jnp.sum(acc, axis=0, keepdims=True)
        return 0

    lax.fori_loop(0, 4, block, 0, unroll=2)


def spread(values, out, first=0):
    for q in range(values.shape[0]):
        rows = pl.ds(first + q * 128, 128)
        out[rows, :] = jnp.broadcast_to(values[q : q + 1, :], (128, 128)).T


def column_half(scores, f_rows, half):
    def peaks(i, carry):
        r = pl.multiple_of(half * 512 + i * 8, 8)
        f = f_rows[pl.ds(r, 8), :]
        return tuple(
            jnp.maximum(carry[k], scores[pl.ds(r, 8), pl.ds(128 * k, 128)] + f)
            for k in range(8)
        )

    start = tuple(jnp.full((8, 128), -1e30, F32) for _ in range(8))
    top = lax.fori_loop(0, 64, peaks, start, unroll=16)
    top = [jnp.broadcast_to(jnp.max(t, axis=0, keepdims=True), (8, 128)) for t in top]

    def sums(i, carry):
        r = pl.multiple_of(half * 512 + i * 8, 8)
        f = f_rows[pl.ds(r, 8), :]
        return tuple(
            carry[k] + jnp.exp2(scores[pl.ds(r, 8), pl.ds(128 * k, 128)] + f - top[k])
            for k in range(8)
        )

    start = tuple(jnp.zeros((8, 128), F32) for _ in range(8))
    return top, lax.fori_loop(0, 64, sums, start, unroll=16)


def join_columns(first, second, out):
    for k in range(8):
        peak = jnp.maximum(first[0][k], second[0][k])
        total = first[1][k] * jnp.exp2(first[0][k] - peak)
        total = total + second[1][k] * jnp.exp2(second[0][k] - peak)
        out[k : k + 1, :] = peak[0:1] + jnp.log2(jnp.sum(total, axis=0, keepdims=True))


def kernel(
    source_ref, target_ref, a_ref, b_ref, readout_out, f_out, g_out,
    readout_ref, f_ref, g_ref,
    sources, targets, masses, b_buf, scores, f_rows, mass_rows, row_buf, column_buf, g_buf, order,
    weights_a, weights_b, partial, arrived, arrived_mass,
    load, own_send, own_recv, far_send, far_recv, y_send, y_recv, in_send, in_recv,
    row_send, row_recv, column_send, column_recv, g_send, g_recv, out_send, out_recv, store,
):
    at = place()
    x, y, z, c = at
    rows, columns = row_peers(at), column_peers(at)
    own = Gather(targets, pl.ds(0, 1), at, own_send, own_recv)
    far = Gather(targets, pl.ds(1, 3), at, far_send, far_recv)
    own_rows = pl.ds(pl.multiple_of((own.u * 4 + own.v) * 64, 64), 64)
    half_rows = pl.ds(pl.multiple_of(c * 512, 512), 512)
    own_target = targets.at[0, own_rows]
    loads = [
        pltpu.make_async_copy(target_ref, own_target, load.at[0]),
        pltpu.make_async_copy(a_ref, masses.at[c], load.at[1]),
        pltpu.make_async_copy(b_ref, b_buf, load.at[2]),
        pltpu.make_async_copy(source_ref, sources.at[half_rows], load.at[3]),
    ]
    for copy in loads:
        copy.start()
    barrier = pltpu.get_barrier_semaphore()
    for peer in columns + rows:
        pl.semaphore_signal(barrier, inc=1, device_id=device(*peer), device_id_type=MESH)
    pl.semaphore_wait(barrier, len(columns) + len(rows))

    sibling = (x, y, z, 1 - c)
    loads[0].wait()
    own.first()
    own.second(0)
    inner = [
        remote(source_ref, sources.at[half_rows], in_send.at[0], in_recv.at[0], sibling),
        remote(a_ref, masses.at[c], in_send.at[1], in_recv.at[1], sibling),
    ]
    for copy in inner:
        copy.start()
    crossings = []
    for k, step in enumerate((1, 3, 2)):
        dst = targets.at[4 - step, own_rows]
        copy = remote(own_target, dst, y_send.at[k], y_recv.at[k], (x, (y + step) % 4, z, c))
        copy.start()
        crossings.append(copy)
    for copy in loads[1:]:
        copy.wait()

    left = lax.broadcasted_iota(jnp.int32, (8, 128), 1) < 64
    for k in range(16):
        turned = k % 4 * 4 + k // 4
        order[0, k : k + 1, :] = jnp.where(
            c == 0, b_buf[k : k + 1, :], b_buf[turned : turned + 1, :]
        )
    even, odd = order[0, pl.ds(0, 8, stride=2), :], order[0, pl.ds(1, 8, stride=2), :]
    log_b = jnp.log2(
        jnp.where(
            c == 0,
            jnp.where(left, even, pltpu.roll(odd, 64, 1)),
            jnp.where(left, pltpu.roll(even, 64, 1), odd),
        )
    )

    def block_scores(plane, at_column):
        columns_at = pl.ds(at_column, 256)
        product = lax.dot_general(
            sources[...], targets[plane, columns_at, :], NT, preferred_element_type=F32
        )
        scores[plane, :, columns_at] = product * SCALE

    zeros = jnp.zeros((8, 128), F32)

    def own_block(k, du):
        column = own.arrived(du)
        block_scores(0, column)

    def far_block(du):
        column = far.arrived(du)

        def one(plane, _):
            block_scores(plane, column)
            return 0

        lax.fori_loop(1, 4, one, 0)

    own.first_forward()
    own.second(3)
    own.second(1)
    own.second_forward(0)
    own.second(2)
    own.second_forward(3)
    own.second_forward(1)
    for copy in inner:
        copy.wait_recv()
    log_a = jnp.log2(jnp.concatenate([masses[0], masses[1]], axis=0))
    own_block(0, 0)
    own.second_forward(2)
    for copy in crossings:
        copy.wait_recv()
    own_block(1, 3)
    far.first()
    own_block(2, 1)
    own_block(3, 2)
    far.second(0)

    def exchange(buf, me, peers, send, recv):
        for peer in peers:
            remote(buf.at[me], buf.at[me], send, recv, peer).start()

    def drain(buf, peers, sem):
        every = buf.at[pl.ds(0, len(peers))]
        pltpu.make_async_copy(every, every, sem).wait()

    def sent(it):
        for h in (0, 1):
            drain(row_buf.at[it, h], rows, row_send.at[it, h])
        drain(column_buf.at[it], columns, column_send.at[it])

    def after_row_send(it):
        if it == 1:
            own.finish()
            for copy in inner + crossings:
                copy.wait_send()
            sent(0)
        if it == 0:
            far.first_forward()
        if it == 1:
            far.second_forward(0)
        if it == 2:
            far.second_forward(2)
            far_block(3)

    def after_column_send(it):
        if it == 0:
            far.second(3)
            far.second(1)
        if it == 1:
            far.second_forward(3)
            far.second(2)
            far.second_forward(1)
            far_block(0)
        if it == 2:
            far_block(1)
            far_block(2)

    g = zeros
    row_me, column_me = y * 2 + c, x * 4 + z
    for it in range(ITERS):
        for h in (0, 1):
            row_pass(scores.at[0], g, h, row_buf.at[it, h, row_me])
            exchange(row_buf.at[it, h], row_me, rows, row_send.at[it, h], row_recv.at[it, h])
        after_row_send(it)
        halves, lses, fs = [], [], []
        for h in (0, 1):
            drain(row_buf.at[it, h], rows, row_recv.at[it, h])
            lses.append(combine([row_buf[it, h, k] for k in range(8)]))
            fs.append(log_a[h * 4 : h * 4 + 4] - lses[h])
            spread(fs[h], f_rows, h * 512)
            halves.append(column_half(scores.at[0], f_rows, h))
        lse, f = jnp.concatenate(lses, axis=0), jnp.concatenate(fs, axis=0)
        join_columns(*halves, column_buf.at[it, column_me])
        exchange(column_buf.at[it], column_me, columns, column_send.at[it], column_recv.at[it])
        after_column_send(it)
        drain(column_buf.at[it], columns, column_recv.at[it])
        g = log_b - combine([column_buf[it, k] for k in range(16)])

    g_buf[0] = g
    shared = []
    for k, step in enumerate((2, 1, 3)):
        to = (x, (y + step) % 4, z, c)
        shared.append(remote(g_buf.at[0], g_buf.at[4 - step], g_send.at[k], g_recv.at[k], to))
    shared.append(remote(g_buf.at[0], g_buf.at[4], g_send.at[3], g_recv.at[3], sibling))
    for copy in shared:
        copy.start()

    spread(-lse, f_rows)
    other = pl.multiple_of((1 - c) * 512, 512)
    mine = pl.multiple_of(c * 512, 512)

    def weigh(start, plane, low):
        shifts = [g_buf[plane, q : q + 1, :] for q in range(8)]
        for i in range(32):
            r = pl.multiple_of(start + i * 16, 16)
            base = f_rows[pl.ds(r, 16), :]
            parts = [
                jnp.exp2(scores[plane, pl.ds(r, 16), q * 128 : (q + 1) * 128] + base + shifts[q])
                for q in range(8)
            ]
            mass = functools.reduce(jnp.add, parts)
            if plane:
                mass = mass + mass_rows[pl.ds(r, 16), :]
            mass_rows[pl.ds(r, 16), :] = mass
            for q in range(8):
                low[i * 16 : (i + 1) * 16, q * 128 : (q + 1) * 128] = parts[q].astype(jnp.bfloat16)

    def product(plane, low, out):
        value = jnp.dot(low[...], targets[plane], preferred_element_type=F32)
        out[...] = out[...] + value if plane else value

    weigh(other, 0, weights_a)
    product(0, weights_a, partial)
    weigh(mine, 0, weights_b)
    for it in (1, 2):
        sent(it)
    far.finish()
    for copy in shared:
        copy.wait_recv()
    product(0, weights_b, readout_ref)
    weigh(other, 1, weights_a)
    product(1, weights_a, partial)
    weigh(other, 2, weights_b)
    product(2, weights_b, partial)
    weigh(other, 3, weights_a)
    product(3, weights_a, partial)
    outward = [
        remote(partial, arrived, out_send.at[0], out_recv.at[0], sibling),
        remote(
            mass_rows.at[pl.ds(other, 512)], arrived_mass, out_send.at[1], out_recv.at[1], sibling
        ),
    ]
    for copy in outward:
        copy.start()

    f_ref[...] = jnp.where(c == 0, f[0:4], f[4:8]) * LN2
    here, there = g_buf[0] * LN2, g_buf[4] * LN2
    g0, g1 = jnp.where(c == 0, here, there), jnp.where(c == 0, there, here)
    order[0, pl.ds(0, 8, stride=2), :] = pltpu.roll(g1, 64, 1)
    order[0, pl.ds(1, 8, stride=2), :] = g1
    order[1, pl.ds(0, 8, stride=2), :] = g0
    order[1, pl.ds(1, 8, stride=2), :] = pltpu.roll(g0, 64, 1)
    for k in range(16):
        turned = k % 4 * 4 + k // 4
        g_ref[k : k + 1, :] = jnp.where(
            left[0:1], order[1, k : k + 1, :], order[0, turned : turned + 1, :]
        )

    weigh(mine, 1, weights_b)
    product(1, weights_b, readout_ref)
    weigh(mine, 2, weights_a)
    product(2, weights_a, readout_ref)
    weigh(mine, 3, weights_b)
    product(3, weights_b, readout_ref)
    for copy in outward:
        copy.wait_recv()
    stores = [
        pltpu.make_async_copy(f_ref, f_out, store.at[4]),
        pltpu.make_async_copy(g_ref, g_out, store.at[5]),
    ]
    for copy in stores:
        copy.start()
    for k in range(4):
        part = pl.ds(k * 128, 128)
        mass = mass_rows[pl.ds(pl.multiple_of(mine + k * 128, 128), 128), :] + arrived_mass[part, :]
        readout_ref[part, :] = (readout_ref[part, :] + arrived[part, :]) * (
            1.0 / jnp.sum(mass, axis=1, keepdims=True)
        )
        copy = pltpu.make_async_copy(readout_ref.at[part], readout_out.at[part], store.at[k])
        copy.start()
        stores.append(copy)

    for copy in shared + outward:
        copy.wait_send()
    for copy in stores:
        copy.wait()


def finish(readout, f, g, readout_out, f_out, g_out, held, held_f, held_g, load, store):
    pairs = [(f, held_f, f_out), (g, held_g, g_out)]
    for k in range(8):
        part = pl.ds(k * 64, 64)
        pairs.append((readout.at[part], held.at[part], readout_out.at[part]))
    loads = [pltpu.make_async_copy(a, b, load.at[k]) for k, (a, b, _) in enumerate(pairs)]
    stores = [pltpu.make_async_copy(b, o, store.at[k]) for k, (_, b, o) in enumerate(pairs)]
    for copy in loads:
        copy.start()
    for before, after in zip(loads, stores):
        before.wait()
        after.start()
    for copy in stores:
        copy.wait()


def shards(source_embed, target_embed, source_mass, target_mass):
    vmem, dma = pltpu.VMEM, pltpu.SemaphoreType.DMA
    bf16 = jnp.bfloat16
    readout, f, g = pl.pallas_call(
        kernel,
        out_shape=(
            jax.ShapeDtypeStruct((512, D), F32),
            jax.ShapeDtypeStruct((4, 128), F32),
            jax.ShapeDtypeStruct((16, 128), F32),
        ),
        in_specs=[pl.BlockSpec(memory_space=pltpu.HBM)] * 4,
        out_specs=(pl.BlockSpec(memory_space=pltpu.HBM),) * 3,
        scratch_shapes=[
            vmem((512, D), F32),
            vmem((4, 128), F32),
            vmem((16, 128), F32),
            vmem((1024, D), bf16),
            vmem((4, 1024, D), bf16),
            vmem((2, 4, 128), F32),
            vmem((16, 128), F32),
            vmem((4, 1024, 1024), F32),
            vmem((1024, 128), F32),
            vmem((1024, 128), F32),
            vmem((ITERS, 2, 8, 4, 128), F32),
            vmem((ITERS, 16, 8, 128), F32),
            vmem((5, 8, 128), F32),
            vmem((5, 16, 128), F32),
            vmem((512, 1024), bf16),
            vmem((512, 1024), bf16),
            vmem((512, D), F32),
            vmem((512, D), F32),
            vmem((512, 128), F32),
            dma((4,)),
            dma((5, 6)),
            dma((5, 6)),
            dma((5, 6)),
            dma((5, 6)),
            dma((3,)),
            dma((3,)),
            dma((2,)),
            dma((2,)),
            dma((ITERS, 2)),
            dma((ITERS, 2)),
            dma((ITERS,)),
            dma((ITERS,)),
            dma((4,)),
            dma((4,)),
            dma((2,)),
            dma((2,)),
            dma((6,)),
        ],
        name="sinkhorn",
        compiler_params=pltpu.CompilerParams(
            collective_id=0, has_side_effects=True, vmem_limit_bytes=56 << 20
        ),
    )(source_embed, target_embed, source_mass.reshape(4, 128), target_mass.reshape(16, 128))
    readout, f, g = pl.pallas_call(
        finish,
        out_shape=(
            jax.ShapeDtypeStruct((512, D), F32),
            jax.ShapeDtypeStruct((4, 128), F32),
            jax.ShapeDtypeStruct((16, 128), F32),
        ),
        in_specs=[pl.BlockSpec(memory_space=pl.ANY)] * 3,
        out_specs=(pl.BlockSpec(memory_space=pl.ANY),) * 3,
        scratch_shapes=[
            vmem((512, D), F32),
            vmem((4, 128), F32),
            vmem((16, 128), F32),
            dma((10,)),
            dma((10,)),
        ],
        name="finish",
        compiler_params=pltpu.CompilerParams(vmem_limit_bytes=60 << 20),
    )(readout, f, g)
    return readout, f.reshape(512), g.reshape(2048)


def solution(mesh):
    placed = (P("src", None), P(("tgt", "src"), None), P("src"), P("tgt"))
    return jax.shard_map(
        shards,
        mesh=mesh,
        in_specs=placed,
        out_specs=(P("src", None), P("src"), P("tgt")),
        check_vma=False,
    )
```

```python
import functools
import math

import jax
import jax.numpy as jnp
from jax import lax
from jax.experimental import pallas as pl
from jax.experimental.pallas import tpu as pltpu
from jax.sharding import PartitionSpec as P

D = 768
ITERS = 3
MESH = pl.DeviceIdType.MESH
SCALE = 2.0 / math.sqrt(D) * math.log2(math.e)
LN2 = math.log(2.0)
NT = (((1,), (1,)), ((), ()))
F32 = jnp.float32


def place():
    s = lax.axis_index("src")
    return s // 8, lax.axis_index("tgt"), (s // 2) % 4, s % 2


def device(x, y, z, c):
    return ((x * 4 + z) * 2 + c, y)


def row_peers(at):
    x, y, z, c = at
    peers = [
        (x, (y + step) % 4, z, (c + other) % 2) for step in (2, 1, 3) for other in (1, 0)
    ]
    return peers + [(x, y, z, 1 - c)]


def column_peers(at):
    x, y, z, c = at
    steps = [(a, b) for a in range(4) for b in range(4) if a or b]
    steps.sort(key=lambda t: -(min(t[0], 4 - t[0]) + min(t[1], 4 - t[1])))
    return [((x + a) % 4, y, (z + b) % 4, c) for a, b in steps]


def remote(src, dst, send, recv, to):
    return pltpu.make_async_remote_copy(
        src_ref=src,
        dst_ref=dst,
        send_sem=send,
        recv_sem=recv,
        device_id=device(*to),
        device_id_type=MESH,
    )


class Gather:
    def __init__(self, targets, planes, at, send, recv):
        self.targets, self.planes = targets, planes
        self.x, self.y, self.z, self.c = at
        self.u = self.x * (1 - self.c) + self.z * self.c
        self.v = self.z * (1 - self.c) + self.x * self.c
        self.send, self.recv = send, recv
        self.copies = {}

    def shift(self, du, dv):
        x = (self.x + du * (1 - self.c) + dv * self.c) % 4
        z = (self.z + du * self.c + dv * (1 - self.c)) % 4
        return (x, self.y, z, self.c)

    def go(self, stage, k, du, dv, low, to):
        row = ((self.u + du) % 4 * 4 + (self.v + dv) % 4) * 64 + low
        block = self.targets.at[self.planes, pl.ds(pl.multiple_of(row, 32), 32), :]
        copy = remote(block, block, self.send.at[stage, k], self.recv.at[stage, k], to)
        copy.start()
        self.copies[stage, k] = copy

    def both_ways(self, stage, du, up, down):
        self.go(stage, 0, du, 0, 0, up)
        self.go(stage, 2, du, 0, 32, down)
        self.go(stage, 1, du, 0, 32, up)
        self.go(stage, 3, du, 0, 0, down)

    def first(self):
        self.both_ways(4, 0, self.shift(1, 0), self.shift(3, 0))

    def first_forward(self):
        self.copies[4, 0].wait_recv()
        self.go(4, 4, 3, 0, 0, self.shift(1, 0))
        self.copies[4, 2].wait_recv()
        self.go(4, 5, 1, 0, 32, self.shift(3, 0))

    def second(self, du):
        if du == 3:
            self.copies[4, 1].wait_recv()
        if du == 1:
            self.copies[4, 3].wait_recv()
        if du == 2:
            self.copies[4, 4].wait_recv()
            self.copies[4, 5].wait_recv()
        self.both_ways(du, du, self.shift(0, 1), self.shift(0, 3))

    def second_forward(self, du):
        self.copies[du, 0].wait_recv()
        self.go(du, 4, du, 3, 0, self.shift(0, 1))
        self.copies[du, 2].wait_recv()
        self.go(du, 5, du, 1, 32, self.shift(0, 3))

    def arrived(self, du):
        for k in (1, 3, 4, 5):
            self.copies[du, k].wait_recv()
        return pl.multiple_of((self.u + du) % 4 * 256, 256)

    def finish(self):
        for copy in self.copies.values():
            copy.wait_send()


def combine(parts):
    peak = functools.reduce(jnp.maximum, parts)
    return peak + jnp.log2(functools.reduce(jnp.add, [jnp.exp2(p - peak) for p in parts]))


def row_pass(scores, g, half, out):
    lane = lax.broadcasted_iota(jnp.int32, (8, 128), 1)
    sub = lax.broadcasted_iota(jnp.int32, (8, 128), 0)
    shifts = [jnp.broadcast_to(g[k : k + 1, :], (8, 128)) for k in range(8)]

    def block(q, _):
        def group(i, acc):
            r = pl.multiple_of(half * 512 + q * 128 + i * 8, 8)
            xs = [scores[pl.ds(r, 8), pl.ds(128 * k, 128)] + shifts[k] for k in range(8)]
            peak = jnp.max(functools.reduce(jnp.maximum, xs), axis=1, keepdims=True)
            total = functools.reduce(jnp.add, [jnp.exp2(x - peak) for x in xs])
            value = peak + jnp.log2(jnp.sum(total, axis=1, keepdims=True))
            return jnp.where(lane - i * 8 == sub, value, acc)

        acc = lax.fori_loop(0, 16, group, jnp.zeros((8, 128), F32), unroll=16)
        out[pl.ds(q, 1), :] = jnp.sum(acc, axis=0, keepdims=True)
        return 0

    lax.fori_loop(0, 4, block, 0, unroll=4)


def spread(values, out, first=0):
    for q in range(values.shape[0]):
        rows = pl.ds(first + q * 128, 128)
        out[rows, :] = jnp.broadcast_to(values[q : q + 1, :], (128, 128)).T


def column_half(scores, f_rows, half):
    def peaks(i, carry):
        r = pl.multiple_of(half * 512 + i * 8, 8)
        f = f_rows[pl.ds(r, 8), :]
        return tuple(
            jnp.maximum(carry[k], scores[pl.ds(r, 8), pl.ds(128 * k, 128)] + f)
            for k in range(8)
        )

    start = tuple(jnp.full((8, 128), -1e30, F32) for _ in range(8))
    top = lax.fori_loop(0, 64, peaks, start, unroll=64)
    top = [jnp.broadcast_to(jnp.max(t, axis=0, keepdims=True), (8, 128)) for t in top]

    def sums(i, carry):
        r = pl.multiple_of(half * 512 + i * 8, 8)
        f = f_rows[pl.ds(r, 8), :]
        return tuple(
            carry[k] + jnp.exp2(scores[pl.ds(r, 8), pl.ds(128 * k, 128)] + f - top[k])
            for k in range(8)
        )

    start = tuple(jnp.zeros((8, 128), F32) for _ in range(8))
    return top, lax.fori_loop(0, 64, sums, start, unroll=64)


def join_columns(first, second, out):
    for k in range(8):
        peak = jnp.maximum(first[0][k], second[0][k])
        total = first[1][k] * jnp.exp2(first[0][k] - peak)
        total = total + second[1][k] * jnp.exp2(second[0][k] - peak)
        out[k : k + 1, :] = peak[0:1] + jnp.log2(jnp.sum(total, axis=0, keepdims=True))


def kernel(
    source_ref, target_ref, a_ref, b_ref, readout_out, f_out, g_out,
    readout_ref, f_ref, g_ref,
    sources, targets, masses, b_buf, scores, f_rows, mass_rows, row_buf, column_buf, g_buf, order,
    weights_a, weights_b, partial, arrived, arrived_mass,
    load, own_send, own_recv, far_send, far_recv, y_send, y_recv, in_send, in_recv,
    row_send, row_recv, column_send, column_recv, g_send, g_recv, out_send, out_recv, store,
):
    at = place()
    x, y, z, c = at
    rows, columns = row_peers(at), column_peers(at)
    own = Gather(targets, pl.ds(0, 1), at, own_send, own_recv)
    far = Gather(targets, pl.ds(1, 3), at, far_send, far_recv)
    own_rows = pl.ds(pl.multiple_of((own.u * 4 + own.v) * 64, 64), 64)
    half_rows = pl.ds(pl.multiple_of(c * 512, 512), 512)
    own_target = targets.at[0, own_rows]
    loads = [
        pltpu.make_async_copy(target_ref, own_target, load.at[0]),
        pltpu.make_async_copy(a_ref, masses.at[c], load.at[1]),
        pltpu.make_async_copy(b_ref, b_buf, load.at[2]),
        pltpu.make_async_copy(source_ref, sources.at[half_rows], load.at[3]),
    ]
    for copy in loads:
        copy.start()
    barrier = pltpu.get_barrier_semaphore()
    for peer in columns + rows:
        pl.semaphore_signal(barrier, inc=1, device_id=device(*peer), device_id_type=MESH)
    pl.semaphore_wait(barrier, len(columns) + len(rows))

    sibling = (x, y, z, 1 - c)
    loads[0].wait()
    own.first()
    own.second(0)
    inner = [
        remote(source_ref, sources.at[half_rows], in_send.at[0], in_recv.at[0], sibling),
        remote(a_ref, masses.at[c], in_send.at[1], in_recv.at[1], sibling),
    ]
    for copy in inner:
        copy.start()
    crossings = []
    for k, step in enumerate((1, 3, 2)):
        dst = targets.at[4 - step, own_rows]
        copy = remote(own_target, dst, y_send.at[k], y_recv.at[k], (x, (y + step) % 4, z, c))
        copy.start()
        crossings.append(copy)
    for copy in loads[1:]:
        copy.wait()

    left = lax.broadcasted_iota(jnp.int32, (8, 128), 1) < 64
    for k in range(16):
        turned = k % 4 * 4 + k // 4
        order[0, k : k + 1, :] = jnp.where(
            c == 0, b_buf[k : k + 1, :], b_buf[turned : turned + 1, :]
        )
    even, odd = order[0, pl.ds(0, 8, stride=2), :], order[0, pl.ds(1, 8, stride=2), :]
    log_b = jnp.log2(
        jnp.where(
            c == 0,
            jnp.where(left, even, pltpu.roll(odd, 64, 1)),
            jnp.where(left, pltpu.roll(even, 64, 1), odd),
        )
    )

    def block_scores(plane, at_column):
        columns_at = pl.ds(at_column, 256)
        product = lax.dot_general(
            sources[...], targets[plane, columns_at, :], NT, preferred_element_type=F32
        )
        scores[plane, :, columns_at] = product * SCALE

    zeros = jnp.zeros((8, 128), F32)

    def own_block(k, du):
        column = own.arrived(du)
        block_scores(0, column)

    def far_block(du):
        column = far.arrived(du)

        def one(plane, _):
            block_scores(plane, column)
            return 0

        lax.fori_loop(1, 4, one, 0)

    own.first_forward()
    own.second(3)
    own.second(1)
    own.second_forward(0)
    own.second(2)
    own.second_forward(3)
    own.second_forward(1)
    for copy in inner:
        copy.wait_recv()
    log_a = jnp.log2(jnp.concatenate([masses[0], masses[1]], axis=0))
    own_block(0, 0)
    own.second_forward(2)
    for copy in crossings:
        copy.wait_recv()
    own_block(1, 3)
    far.first()
    own_block(2, 1)
    own_block(3, 2)
    far.second(0)

    def exchange(buf, me, peers, send, recv):
        for peer in peers:
            remote(buf.at[me], buf.at[me], send, recv, peer).start()

    def drain(buf, peers, sem):
        every = buf.at[pl.ds(0, len(peers))]
        pltpu.make_async_copy(every, every, sem).wait()

    def sent(it):
        for h in (0, 1):
            drain(row_buf.at[it, h], rows, row_send.at[it, h])
        drain(column_buf.at[it], columns, column_send.at[it])

    def after_row_send(it):
        if it == 1:
            own.finish()
            for copy in inner + crossings:
                copy.wait_send()
            sent(0)
        if it == 0:
            far.first_forward()
        if it == 1:
            far.second_forward(0)
        if it == 2:
            far.second_forward(2)
            far_block(3)

    def after_column_send(it):
        if it == 0:
            far.second(3)
            far.second(1)
        if it == 1:
            far.second_forward(3)
            far.second(2)
            far.second_forward(1)
            far_block(0)
        if it == 2:
            far_block(1)
            far_block(2)

    g = zeros
    row_me, column_me = y * 2 + c, x * 4 + z
    for it in range(ITERS):
        for h in (0, 1):
            row_pass(scores.at[0], g, h, row_buf.at[it, h, row_me])
            exchange(row_buf.at[it, h], row_me, rows, row_send.at[it, h], row_recv.at[it, h])
        after_row_send(it)
        halves, lses, fs = [], [], []
        for h in (0, 1):
            drain(row_buf.at[it, h], rows, row_recv.at[it, h])
            lses.append(combine([row_buf[it, h, k] for k in range(8)]))
            fs.append(log_a[h * 4 : h * 4 + 4] - lses[h])
            spread(fs[h], f_rows, h * 512)
            halves.append(column_half(scores.at[0], f_rows, h))
        lse, f = jnp.concatenate(lses, axis=0), jnp.concatenate(fs, axis=0)
        join_columns(*halves, column_buf.at[it, column_me])
        exchange(column_buf.at[it], column_me, columns, column_send.at[it], column_recv.at[it])
        after_column_send(it)
        drain(column_buf.at[it], columns, column_recv.at[it])
        g = log_b - combine([column_buf[it, k] for k in range(16)])

    g_buf[0] = g
    shared = []
    for k, step in enumerate((2, 1, 3)):
        to = (x, (y + step) % 4, z, c)
        shared.append(remote(g_buf.at[0], g_buf.at[4 - step], g_send.at[k], g_recv.at[k], to))
    shared.append(remote(g_buf.at[0], g_buf.at[4], g_send.at[3], g_recv.at[3], sibling))
    for copy in shared:
        copy.start()

    spread(-lse, f_rows)
    other = pl.multiple_of((1 - c) * 512, 512)
    mine = pl.multiple_of(c * 512, 512)

    def weigh(start, plane, low):
        shifts = [g_buf[plane, q : q + 1, :] for q in range(8)]
        for i in range(32):
            r = pl.multiple_of(start + i * 16, 16)
            base = f_rows[pl.ds(r, 16), :]
            parts = [
                jnp.exp2(scores[plane, pl.ds(r, 16), q * 128 : (q + 1) * 128] + base + shifts[q])
                for q in range(8)
            ]
            mass = functools.reduce(jnp.add, parts)
            if plane:
                mass = mass + mass_rows[pl.ds(r, 16), :]
            mass_rows[pl.ds(r, 16), :] = mass
            for q in range(8):
                low[i * 16 : (i + 1) * 16, q * 128 : (q + 1) * 128] = parts[q].astype(jnp.bfloat16)

    def product(plane, low, out):
        value = jnp.dot(low[...], targets[plane], preferred_element_type=F32)
        out[...] = out[...] + value if plane else value

    weigh(other, 0, weights_a)
    product(0, weights_a, partial)
    weigh(mine, 0, weights_b)
    for it in (1, 2):
        sent(it)
    far.finish()
    for copy in shared:
        copy.wait_recv()
    product(0, weights_b, readout_ref)
    weigh(other, 1, weights_a)
    product(1, weights_a, partial)
    weigh(other, 2, weights_b)
    product(2, weights_b, partial)
    weigh(other, 3, weights_a)
    product(3, weights_a, partial)
    outward = [
        remote(partial, arrived, out_send.at[0], out_recv.at[0], sibling),
        remote(
            mass_rows.at[pl.ds(other, 512)], arrived_mass, out_send.at[1], out_recv.at[1], sibling
        ),
    ]
    for copy in outward:
        copy.start()

    f_ref[...] = jnp.where(c == 0, f[0:4], f[4:8]) * LN2
    here, there = g_buf[0] * LN2, g_buf[4] * LN2
    g0, g1 = jnp.where(c == 0, here, there), jnp.where(c == 0, there, here)
    order[0, pl.ds(0, 8, stride=2), :] = pltpu.roll(g1, 64, 1)
    order[0, pl.ds(1, 8, stride=2), :] = g1
    order[1, pl.ds(0, 8, stride=2), :] = g0
    order[1, pl.ds(1, 8, stride=2), :] = pltpu.roll(g0, 64, 1)
    for k in range(16):
        turned = k % 4 * 4 + k // 4
        g_ref[k : k + 1, :] = jnp.where(
            left[0:1], order[1, k : k + 1, :], order[0, turned : turned + 1, :]
        )

    weigh(mine, 1, weights_b)
    product(1, weights_b, readout_ref)
    weigh(mine, 2, weights_a)
    product(2, weights_a, readout_ref)
    weigh(mine, 3, weights_b)
    product(3, weights_b, readout_ref)
    for copy in outward:
        copy.wait_recv()
    stores = [
        pltpu.make_async_copy(f_ref, f_out, store.at[4]),
        pltpu.make_async_copy(g_ref, g_out, store.at[5]),
    ]
    for copy in stores:
        copy.start()
    for k in range(4):
        part = pl.ds(k * 128, 128)
        mass = mass_rows[pl.ds(pl.multiple_of(mine + k * 128, 128), 128), :] + arrived_mass[part, :]
        readout_ref[part, :] = (readout_ref[part, :] + arrived[part, :]) * (
            1.0 / jnp.sum(mass, axis=1, keepdims=True)
        )
        copy = pltpu.make_async_copy(readout_ref.at[part], readout_out.at[part], store.at[k])
        copy.start()
        stores.append(copy)

    for copy in shared + outward:
        copy.wait_send()
    for copy in stores:
        copy.wait()


def finish(readout, f, g, readout_out, f_out, g_out, held, held_f, held_g, load, store):
    pairs = [(f, held_f, f_out), (g, held_g, g_out)]
    for k in range(8):
        part = pl.ds(k * 64, 64)
        pairs.append((readout.at[part], held.at[part], readout_out.at[part]))
    loads = [pltpu.make_async_copy(a, b, load.at[k]) for k, (a, b, _) in enumerate(pairs)]
    stores = [pltpu.make_async_copy(b, o, store.at[k]) for k, (_, b, o) in enumerate(pairs)]
    for copy in loads:
        copy.start()
    for before, after in zip(loads, stores):
        before.wait()
        after.start()
    for copy in stores:
        copy.wait()


def shards(source_embed, target_embed, source_mass, target_mass):
    vmem, dma = pltpu.VMEM, pltpu.SemaphoreType.DMA
    bf16 = jnp.bfloat16
    readout, f, g = pl.pallas_call(
        kernel,
        out_shape=(
            jax.ShapeDtypeStruct((512, D), F32),
            jax.ShapeDtypeStruct((4, 128), F32),
            jax.ShapeDtypeStruct((16, 128), F32),
        ),
        in_specs=[pl.BlockSpec(memory_space=pltpu.HBM)] * 4,
        out_specs=(pl.BlockSpec(memory_space=pltpu.HBM),) * 3,
        scratch_shapes=[
            vmem((512, D), F32),
            vmem((4, 128), F32),
            vmem((16, 128), F32),
            vmem((1024, D), bf16),
            vmem((4, 1024, D), bf16),
            vmem((2, 4, 128), F32),
            vmem((16, 128), F32),
            vmem((4, 1024, 1024), F32),
            vmem((1024, 128), F32),
            vmem((1024, 128), F32),
            vmem((ITERS, 2, 8, 4, 128), F32),
            vmem((ITERS, 16, 8, 128), F32),
            vmem((5, 8, 128), F32),
            vmem((5, 16, 128), F32),
            vmem((512, 1024), bf16),
            vmem((512, 1024), bf16),
            vmem((512, D), F32),
            vmem((512, D), F32),
            vmem((512, 128), F32),
            dma((4,)),
            dma((5, 6)),
            dma((5, 6)),
            dma((5, 6)),
            dma((5, 6)),
            dma((3,)),
            dma((3,)),
            dma((2,)),
            dma((2,)),
            dma((ITERS, 2)),
            dma((ITERS, 2)),
            dma((ITERS,)),
            dma((ITERS,)),
            dma((4,)),
            dma((4,)),
            dma((2,)),
            dma((2,)),
            dma((6,)),
        ],
        name="sinkhorn",
        compiler_params=pltpu.CompilerParams(
            collective_id=0, has_side_effects=True, vmem_limit_bytes=56 << 20
        ),
    )(source_embed, target_embed, source_mass.reshape(4, 128), target_mass.reshape(16, 128))
    readout, f, g = pl.pallas_call(
        finish,
        out_shape=(
            jax.ShapeDtypeStruct((512, D), F32),
            jax.ShapeDtypeStruct((4, 128), F32),
            jax.ShapeDtypeStruct((16, 128), F32),
        ),
        in_specs=[pl.BlockSpec(memory_space=pl.ANY)] * 3,
        out_specs=(pl.BlockSpec(memory_space=pl.ANY),) * 3,
        scratch_shapes=[
            vmem((512, D), F32),
            vmem((4, 128), F32),
            vmem((16, 128), F32),
            dma((10,)),
            dma((10,)),
        ],
        name="finish",
        compiler_params=pltpu.CompilerParams(vmem_limit_bytes=60 << 20),
    )(readout, f, g)
    return readout, f.reshape(512), g.reshape(2048)


def solution(mesh):
    placed = (P("src", None), P(("tgt", "src"), None), P("src"), P("tgt"))
    return jax.shard_map(
        shards,
        mesh=mesh,
        in_specs=placed,
        out_specs=(P("src", None), P("src"), P("tgt")),
        check_vma=False,
    )
```
